32 devices in a mesh: groups: 2 (over x), dp: 16 (over z, y, core).
Axes of the slice: x: 2, y: 2, z: 4, core: 2. Of those that a mesh axis runs over, the one named last changes fastest.
Arguments:
- embeddings: bfloat16 [262144, 1024], P(('groups', 'dp')), parts along dimension 0
- cluster_ids: int32 [262144], P(('groups', 'dp')), parts along dimension 0, may hold values from 0 to 15, as said below
- owner_table: int32 [32], P('groups'), parts along dimension 0, may hold values from 0 to 15, each once
- start_basis: float32 [8, 1024], replicated, may hold values from -6 to 6
Outputs:
- directions: float32 [32, 8, 1024], P(('groups', 'dp')), parts along dimension 0
- projections: float32 [8, 262144], P(None, ('groups', 'dp')), parts along dimension 1
The draws below stay inside these ranges and needn't reach their ends.
There are 2 independent parts, one for each index of `groups`. The reference program is written for one: setup_inputs(seed, part) draws one part's arguments, and reference() takes and returns one part's arrays. A program takes and returns all parts, laid end to end along the dimension named above; an argument that names none is the same for every part. Nothing has to cross between parts.
Inputs may be any that keep to these rules, and one draw needn't show every extreme that they name: `cluster_ids`: Sorted. Each cluster's rows form a run whose length is a multiple of 2048, from 2048 to 32768; every cluster has rows and one has exactly 32768. The rows of one device belong to at most 4 clusters, and some device's rows belong to exactly 4. A permutation: index k of dp owns cluster owner_table[k].
All inputs are finite; a program needn't handle non-finite values.
Results may differ from the reference program's by a relative error of at most 0.0075.
Values sent between devices are 32-bit elements; how exact they have to be, the bound alone decides.
No kernel may reach another device: no remote copies, remote signals or barrier semaphores. Data moves between devices by JAX's collectives and lax.ppermute only.
A program may use at most 128 MiB of HBM per device.

```python
import jax
import jax.numpy as jnp
from jax import lax

D = 1024
DIRS = 8
SEGS = 4
ITERS = 6
ROWS_DEV = 8192
CLUSTERS = 16
ROWS = 131072
N_DP = 16


def unit_sizes(key):
    key = jax.random.fold_in(key, 11)
    pair_count = (CLUSTERS - 6) // 2
    size_key, place_key = jax.random.split(key)
    leading = jax.random.randint(size_key, (pair_count,), 1, 8)
    paired = jnp.stack([leading, 8 - leading], axis=1).reshape(-1)
    before = 2 * jax.random.randint(place_key, (), 0, pair_count + 1)
    special = jnp.array([16, 1, 1, 1, 1, 4], dtype=jnp.int32)
    position = jnp.arange(CLUSTERS, dtype=jnp.int32)
    early_pairs = paired[jnp.clip(position, 0, 2 * pair_count - 1)]
    special_part = special[jnp.clip(position - before, 0, 5)]
    late_pairs = paired[jnp.clip(position - 6, 0, 2 * pair_count - 1)]
    chosen = jnp.where(position < before, early_pairs, jnp.where(position < before + 6, special_part, late_pairs))
    return chosen.astype(jnp.int32)


def row_labels(key):
    sizes = unit_sizes(key)
    ends = jnp.cumsum(sizes)
    units = jnp.arange(SEGS * CLUSTERS, dtype=jnp.int32)
    unit_label = jnp.sum((ends[None, :] <= units[:, None]).astype(jnp.int32), axis=1)
    return jnp.repeat(unit_label, ROWS_DEV // SEGS, total_repeat_length=ROWS).astype(jnp.int32)


def draw_cluster_ids(key, part):
    return row_labels(key)


def draw_embeddings(key, part):
    labels = row_labels(key)
    key = jax.random.fold_in(key, 3)
    col_key, row_key, offset_key, noise_key = jax.random.split(key, 4)
    noise = jax.random.normal(noise_key, (ROWS, D), jnp.float32)
    row_scale = jnp.exp(jax.random.uniform(row_key, (ROWS, 1), jnp.float32, jnp.log(0.5), jnp.log(5.0)))
    offsets = 0.7 * jax.random.normal(offset_key, (CLUSTERS, D), jnp.float32)
    col_scale = jnp.exp(jax.random.uniform(col_key, (1, D), jnp.float32, jnp.log(0.5), jnp.log(2.0)))
    values = 0.35 * (noise * row_scale * col_scale + offsets[labels])
    return values.astype(jnp.bfloat16)


def normal_values(stream_key, dims, spread, reach, kind=jnp.bfloat16):
    result = spread * jax.random.normal(stream_key, dims, jnp.float32)
    return jnp.clip(result, min=-reach, max=reach).astype(kind)


def setup_inputs(seed: int = 0, part: int = 0) -> dict:
    arg_keys = jax.random.split(jax.random.key(seed), 5)
    part_splits = jax.random.split(jax.random.fold_in(arg_keys[4], part), 5)
    return {
        "embeddings": draw_embeddings(jax.random.fold_in(jax.random.fold_in(arg_keys[4], part), 71), part),
        "cluster_ids": draw_cluster_ids(jax.random.fold_in(jax.random.fold_in(arg_keys[4], part), 71), part),
        "owner_table": jax.random.permutation(part_splits[2], CLUSTERS).astype(jnp.int32),
        "start_basis": normal_values(arg_keys[3], (DIRS, D), 1.0, 6.0, jnp.float32),
    }


def chol_rows(images):
    gram_matrix = jnp.einsum('bid,bjd->bij', images, images, precision=lax.Precision.HIGHEST)
    lower_factor = jnp.linalg.cholesky(gram_matrix)
    return jax.scipy.linalg.solve_triangular(lower_factor, images, lower=True)

def layout(label_block):
    slot_index = jnp.arange(SEGS, dtype=jnp.int32)
    all_labels = jnp.arange(CLUSTERS, dtype=jnp.int32)
    labels = label_block[0] + slot_index
    member = (label_block[None, :] == labels[:, None]).astype(jnp.float32)
    select = (all_labels[None, :] == labels[:, None]).astype(jnp.float32)
    return (member, select)

def masked_scores(basis, member, select, centered_block):
    narrow = jnp.einsum('jk,kid->jid', select, basis, precision=lax.Precision.HIGHEST)
    narrow = narrow.astype(jnp.bfloat16).reshape(SEGS * DIRS, D)
    scores = jnp.dot(narrow.astype(jnp.float32), centered_block.T.astype(jnp.float32), preferred_element_type=jnp.float32)
    return scores.reshape(SEGS, DIRS, ROWS_DEV) * member[:, None, :]

def reference(embeddings, cluster_ids, owner_table, start_basis):
    row_blocks = embeddings.reshape(N_DP, ROWS_DEV, D)
    label_blocks = cluster_ids.reshape(N_DP, ROWS_DEV)

    def add_stats(carry, blocked):
        row_block, label_block = blocked
        member, select = layout(label_block)
        partial_sums = jnp.dot(member.astype(jnp.bfloat16).astype(jnp.float32), row_block.astype(jnp.float32), preferred_element_type=jnp.float32)
        partial_counts = jnp.sum(member, axis=1)
        return ((carry[0] + jnp.dot(select.T, partial_sums, precision=lax.Precision.HIGHEST), carry[1] + jnp.dot(partial_counts, select, precision=lax.Precision.HIGHEST)), None)
    zero_stats = (jnp.zeros((CLUSTERS, D), jnp.float32), jnp.zeros((CLUSTERS,), jnp.float32))
    (sums, counts), unused = lax.scan(add_stats, zero_stats, (row_blocks, label_blocks))
    cluster_means = sums / counts[:, None]

    def center(blocked):
        row_block, label_block = blocked
        member, select = layout(label_block)
        seg_means = jnp.dot(select, cluster_means, precision=lax.Precision.HIGHEST)
        row_means = jnp.dot(member.T, seg_means, precision=lax.Precision.HIGHEST)
        return (row_block.astype(jnp.float32) - row_means).astype(jnp.bfloat16)
    centered = lax.map(center, (row_blocks, label_blocks))
    basis = jnp.broadcast_to(start_basis, (CLUSTERS, DIRS, D)).astype(jnp.float32)
    for iteration in range(ITERS):

        def add_image(running, blocked):
            centered_block, label_block = blocked
            member, select = layout(label_block)
            scores = masked_scores(basis, member, select, centered_block)
            scores = scores.astype(jnp.bfloat16).reshape(SEGS * DIRS, ROWS_DEV)
            images = jnp.dot(scores.astype(jnp.float32), centered_block.astype(jnp.float32), preferred_element_type=jnp.float32).reshape(SEGS, DIRS, D)
            return (running + jnp.einsum('jk,jid->kid', select, images, precision=lax.Precision.HIGHEST), None)
        images, unused = lax.scan(add_image, jnp.zeros((CLUSTERS, DIRS, D), jnp.float32), (centered, label_blocks))
        basis = chol_rows(images)
    directions = basis[owner_table]

    def project(blocked):
        centered_block, label_block = blocked
        member, select = layout(label_block)
        return jnp.sum(masked_scores(basis, member, select, centered_block), axis=0)
    projected = lax.map(project, (centered, label_blocks))
    projections = jnp.transpose(projected, (1, 0, 2)).reshape(DIRS, N_DP * ROWS_DEV)
    return (directions, projections)
```

```python
import functools

import jax
import jax.numpy as jnp
from jax import lax
from jax.experimental import pallas as pl
from jax.experimental.pallas import tpu as pltpu
from jax.sharding import PartitionSpec as P

DIRS = 8
ITERS = 6
UNIT = 2048
HIGHEST = lax.Precision.HIGHEST
VMEM_LIMIT = 56 * 1024 * 1024


def dot(a, b, contract=((1,), (0,)), precision=None):
    return lax.dot_general(
        a, b, (contract, ((), ())), precision=precision, preferred_element_type=jnp.float32
    )


def means_kernel(x_ref, out_ref):
    out_ref[0] = jnp.sum(x_ref[...].astype(jnp.float32), axis=0, keepdims=True) / UNIT


def unit_means(x):
    rows, width = x.shape
    return pl.pallas_call(
        means_kernel,
        grid=(rows // UNIT,),
        in_specs=[pl.BlockSpec((UNIT, width), lambda u: (u, 0))],
        out_specs=pl.BlockSpec((1, 1, width), lambda u: (u, 0, 0)),
        out_shape=jax.ShapeDtypeStruct((rows // UNIT, 1, width), jnp.float32),
        compiler_params=pltpu.CompilerParams(vmem_limit_bytes=VMEM_LIMIT),
        name="unit_means",
    )(x)


def apply_unit(narrow, high, low):
    return dot(narrow, high) + dot(narrow, low)


def spread_kernel(x_ref, mean_ref, start_ref, high_ref, low_ref, image_ref):
    centered = (x_ref[...].astype(jnp.float32) - mean_ref[0]).astype(jnp.bfloat16)
    spread = dot(centered, centered, ((0,), (0,)))
    high = spread.astype(jnp.bfloat16)
    high_ref[0] = high
    low = (spread - high.astype(jnp.float32)).astype(jnp.bfloat16)
    low_ref[0] = low
    image_ref[0] = apply_unit(start_ref[...].astype(jnp.bfloat16), high, low)


def unit_spread(x, means, start):
    rows, width = x.shape
    units = rows // UNIT
    half = jax.ShapeDtypeStruct((units, width, width), jnp.bfloat16)
    square = pl.BlockSpec((1, width, width), lambda u: (u, 0, 0))
    return pl.pallas_call(
        spread_kernel,
        grid=(units,),
        in_specs=[
            pl.BlockSpec((UNIT, width), lambda u: (u, 0)),
            pl.BlockSpec((1, 1, width), lambda u: (u, 0, 0)),
            pl.BlockSpec((DIRS, width), lambda u: (0, 0)),
        ],
        out_specs=[square, square, pl.BlockSpec((1, DIRS, width), lambda u: (u, 0, 0))],
        out_shape=[half, half, jax.ShapeDtypeStruct((units, DIRS, width), jnp.float32)],
        compiler_params=pltpu.CompilerParams(vmem_limit_bytes=VMEM_LIMIT),
        name="unit_spread",
    )(x, means, start)


def merge_units(images, narrow, shift, same_ref, out_ref):
    units = len(images)
    full = []
    for u in range(units):
        along = jnp.sum(narrow[u].astype(jnp.float32) * shift[u], axis=1, keepdims=True)
        full.append(images[u] + (UNIT * along) * shift[u])
    for u in range(units):
        total = full[u]
        for v in range(units):
            if v != u:
                total = total + full[v] * same_ref[u, v]
        out_ref[u] = total


def first_kernel(same_ref, weight_ref, all_means_ref, means_ref, start_ref, image_ref, out_ref, shift_ref):
    units = means_ref.shape[0]
    cluster_means = dot(weight_ref[...], all_means_ref[...], precision=HIGHEST)
    narrow = start_ref[...].astype(jnp.bfloat16)
    shift = [means_ref[u] - cluster_means[u : u + 1] for u in range(units)]
    for u in range(units):
        shift_ref[u] = shift[u]
    merge_units([image_ref[u] for u in range(units)], [narrow] * units, shift, same_ref, out_ref)


def vmem(count):
    return [pl.BlockSpec(memory_space=pltpu.VMEM)] * count


def smem(count):
    return [pl.BlockSpec(memory_space=pltpu.SMEM)] * count


def first_images(same, weight, all_means, means, start, images):
    units, _, width = means.shape
    return pl.pallas_call(
        first_kernel,
        in_specs=smem(1) + vmem(5),
        out_specs=vmem(2),
        out_shape=[
            jax.ShapeDtypeStruct((units, DIRS, width), jnp.float32),
            jax.ShapeDtypeStruct((units, 1, width), jnp.float32),
        ],
        compiler_params=pltpu.CompilerParams(vmem_limit_bytes=VMEM_LIMIT),
        name="first_images",
    )(same, weight, all_means, means, start, images)


def orthonormal(side_ref, image_ref, first_ref, last_ref):
    units = image_ref.shape[0]
    size = units * DIRS
    first, last = first_ref[...], last_ref[...]
    images = jnp.concatenate(
        [image_ref[u] + first * side_ref[0, u] + last * side_ref[1, u] for u in range(units)], axis=0
    )
    gram = dot(images, images, ((1,), (1,)), HIGHEST)
    row = lax.broadcasted_iota(jnp.int32, (DIRS, size), 0)
    lane = lax.broadcasted_iota(jnp.int32, (DIRS, size), 1)
    inverse = []
    for u in range(units):
        left = gram[u * DIRS : (u + 1) * DIRS]
        right = (lane == row + u * DIRS).astype(jnp.float32)
        for k in range(DIRS - 1):
            c = u * DIRS + k
            factor = jnp.where(row[:, :1] > k, left[:, c : c + 1] / left[k : k + 1, c : c + 1], 0.0)
            right = right - factor * right[k : k + 1]
            left = left - factor * left[k : k + 1]
        diagonal = jnp.sum(jnp.where(lane == row + u * DIRS, left, 0.0), axis=1, keepdims=True)
        inverse.append(right / jnp.sqrt(diagonal))
    return dot(jnp.concatenate(inverse, axis=0), images, precision=HIGHEST)


def step_kernel(same_ref, side_ref, image_ref, first_ref, last_ref, shift_ref, high_ref, low_ref, out_ref):
    units = image_ref.shape[0]
    basis = orthonormal(side_ref, image_ref, first_ref, last_ref).astype(jnp.bfloat16)
    narrow = [basis[u * DIRS : (u + 1) * DIRS] for u in range(units)]
    images = [apply_unit(narrow[u], high_ref[u], low_ref[u]) for u in range(units)]
    merge_units(images, narrow, [shift_ref[u] for u in range(units)], same_ref, out_ref)


def step(same, side, images, first, last, shift, high, low):
    return pl.pallas_call(
        step_kernel,
        in_specs=smem(2) + vmem(6),
        out_specs=vmem(1)[0],
        out_shape=jax.ShapeDtypeStruct(images.shape, jnp.float32),
        compiler_params=pltpu.CompilerParams(vmem_limit_bytes=VMEM_LIMIT),
        name="step",
    )(same, side, images, first, last, shift, high, low)


def last_kernel(side_ref, image_ref, first_ref, last_ref, mean_ref, shift_ref, x_ref, basis_ref, out_ref, narrow):
    units = image_ref.shape[0]
    u = pl.program_id(0)

    @pl.when(u == 0)
    def _():
        basis = orthonormal(side_ref, image_ref, first_ref, last_ref)
        for v in range(units):
            basis_ref[v] = basis[v * DIRS : (v + 1) * DIRS]
            narrow[v] = basis[v * DIRS : (v + 1) * DIRS].astype(jnp.bfloat16)

    chosen = narrow[u]
    cluster_mean = mean_ref[u] - shift_ref[u]
    offset = jnp.sum(chosen.astype(jnp.float32) * cluster_mean, axis=1, keepdims=True)
    out_ref[...] = dot(chosen, x_ref[...], ((1,), (1,))) - offset


def last(side, images, first, last_image, means, shift, x):
    rows, width = x.shape
    units = rows // UNIT
    whole = pl.BlockSpec((units, DIRS, width), lambda u: (0, 0, 0))
    one = pl.BlockSpec((DIRS, width), lambda u: (0, 0))
    line = pl.BlockSpec((units, 1, width), lambda u: (0, 0, 0))
    return pl.pallas_call(
        last_kernel,
        grid=(units,),
        in_specs=smem(1) + [whole, one, one, line, line, pl.BlockSpec((UNIT, width), lambda u: (u, 0))],
        out_specs=[whole, pl.BlockSpec((DIRS, UNIT), lambda u: (0, u))],
        out_shape=[
            jax.ShapeDtypeStruct((units, DIRS, width), jnp.float32),
            jax.ShapeDtypeStruct((DIRS, rows), jnp.float32),
        ],
        scratch_shapes=[pltpu.VMEM((units, DIRS, width), jnp.bfloat16)],
        compiler_params=pltpu.CompilerParams(vmem_limit_bytes=VMEM_LIMIT),
        name="last",
    )(side, images, first, last_image, means, shift, x)


def per_device(n_dp, embeddings, cluster_ids, owner_table, start_basis):
    rows, width = embeddings.shape
    units = rows // UNIT
    chips = n_dp // 2
    me = lax.axis_index("dp")
    chip, core = me // 2, me % 2
    labels = cluster_ids.reshape(units, UNIT)[:, 0]

    means = unit_means(embeddings)
    stats = jnp.concatenate(
        [
            means.reshape(units, width),
            jnp.broadcast_to(labels.astype(jnp.float32)[:, None], (units, width)),
        ]
    )
    high, low, raw = unit_spread(embeddings, means, start_basis)
    stats = lax.all_gather(stats, "dp").reshape(n_dp, 2, units, width)
    all_means = stats[:, 0].reshape(n_dp * units, width)
    all_labels = stats[:, 1, :, 0].astype(jnp.int32)

    match = (labels[:, None] == all_labels.reshape(1, -1)).astype(jnp.float32)
    weight = match / jnp.sum(match, axis=1, keepdims=True)
    same = (labels[:, None] == labels[None, :]).astype(jnp.float32)
    side = jnp.stack([labels == labels[0], labels == labels[-1]]).astype(jnp.float32)

    heads, tails = all_labels[:, 0], all_labels[:, -1]
    head, tail = heads[me], tails[me]
    chip_head, chip_tail = heads[2 * chip], tails[2 * chip + 1]
    mate = me ^ 1

    def flag(value):
        return value.astype(jnp.float32)

    even = core == 0
    join_head = flag(heads[2 * chip + 1] == chip_head)
    join_tail = flag(tails[2 * chip] == chip_tail)
    mate_left = flag((core == 1) & (tails[mate] == head))
    mate_right = flag((core == 0) & (heads[mate] == tail))
    chip_own_head = flag(head == chip_head)
    chip_own_tail = flag(tail == chip_tail)

    near = (lambda p: p ^ 1, lambda p: (p + 1) % chips if p % 2 else (p - 1) % chips)
    far = (lambda p: p ^ 2, lambda p: (p + 2) % chips if p % 4 >= 2 else (p - 2) % chips)
    links = []
    for pairing in (near, far):
        targets = [2 * pairing[c](p) + c for p in range(chips) for c in range(2)]
        other = jnp.asarray([t // 2 for t in targets], jnp.int32)[me]
        up = other > chip
        from_left = flag(~up & (tails[2 * other + 1] == chip_head))
        from_right = flag(up & (heads[2 * other] == chip_tail))
        links.append((list(enumerate(targets)), up, from_left, from_right))
    mates = [(i, i ^ 1) for i in range(n_dp)]

    def swap(a, b):
        both = lax.ppermute(jnp.concatenate([a, b]), "dp", mates)
        return both[:DIRS], both[DIRS:]

    def exchange(images):
        own_head, own_tail = images[0], images[-1]
        mate_head, mate_tail = swap(own_head, own_tail)
        total_head = jnp.where(even, own_head + join_head * mate_head, mate_head + join_head * own_head)
        total_tail = jnp.where(even, mate_tail + join_tail * own_tail, own_tail + join_tail * mate_tail)
        left = right = jnp.zeros_like(own_head)
        for permutation, up, from_left, from_right in links:
            got = lax.ppermute(jnp.where(up, total_tail, total_head), "dp", permutation)
            left = left + from_left * got
            right = right + from_right * got
        mate_side = swap(left, right)
        first = chip_own_head * (left + mate_side[0]) + mate_left * mate_tail
        last_image = chip_own_tail * (right + mate_side[1]) + mate_right * mate_head
        return first, last_image

    images, shift = first_images(same, weight, all_means, means, start_basis, raw)
    for _ in range(ITERS - 1):
        images = step(same, side, images, *exchange(images), shift, high, low)
    basis, projections = last(side, images, *exchange(images), means, shift, embeddings)

    flat = all_labels.reshape(-1)
    starts = jnp.concatenate([jnp.ones((1,), bool), flat[1:] != flat[:-1]]).reshape(n_dp, units)[me]
    pick = (owner_table[:, None] == labels[None, :]) & starts[None, :]
    outgoing = jnp.einsum("ku,uid->kid", pick.astype(jnp.float32), basis, precision=HIGHEST)
    arrived = lax.all_to_all(outgoing, "dp", 0, 0, tiled=True)
    return jnp.sum(arrived, axis=0, keepdims=True), projections


def solution(mesh):
    in_specs = (P(("groups", "dp"), None), P(("groups", "dp")), P("groups"), P())
    out_specs = (P(("groups", "dp"), None, None), P(None, ("groups", "dp")))
    body = functools.partial(per_device, mesh.shape["dp"])
    return jax.shard_map(body, mesh=mesh, in_specs=in_specs, out_specs=out_specs, check_vma=False)
```

```python
import functools

import jax
import jax.numpy as jnp
from jax import lax
from jax.experimental import pallas as pl
from jax.experimental.pallas import tpu as pltpu
from jax.sharding import PartitionSpec as P

DIRS = 8
ITERS = 6
UNIT = 2048
HIGHEST = lax.Precision.HIGHEST
MIB = 1024 * 1024


def dot(a, b, contract=((1,), (0,)), precision=None):
    return lax.dot_general(
        a, b, (contract, ((), ())), precision=precision, preferred_element_type=jnp.float32
    )


def means_kernel(parts, x_ref, out_ref):
    part = jnp.sum(x_ref[...].astype(jnp.float32), axis=0, keepdims=True) * (1 / UNIT)

    @pl.when(pl.program_id(1) == 0)
    def _():
        out_ref[0] = part

    @pl.when(pl.program_id(1) > 0)
    def _():
        out_ref[0] += part


def unit_means(x, parts=4):
    rows, width = x.shape
    return pl.pallas_call(
        functools.partial(means_kernel, parts),
        grid=(rows // UNIT, parts),
        in_specs=[pl.BlockSpec((UNIT // parts, width), lambda u, p: (u * parts + p, 0))],
        out_specs=pl.BlockSpec((1, 1, width), lambda u, p: (u, 0, 0)),
        out_shape=jax.ShapeDtypeStruct((rows // UNIT, 1, width), jnp.float32),
        compiler_params=pltpu.CompilerParams(vmem_limit_bytes=8 * MIB),
        name="unit_means",
    )(x)


def apply_unit(narrow, high, low):
    return dot(narrow, high) + dot(narrow, low)


def spread_kernel(x_ref, mean_ref, start_ref, high_ref, low_ref, image_ref):
    u = pl.program_id(0)
    centered = (x_ref[...].astype(jnp.float32) - mean_ref[0]).astype(jnp.bfloat16)
    spread = dot(centered, centered, ((0,), (0,)))
    high = spread.astype(jnp.bfloat16)
    high_ref[u] = high
    low = (spread - high.astype(jnp.float32)).astype(jnp.bfloat16)
    low_ref[u] = low
    image_ref[u] = apply_unit(start_ref[...].astype(jnp.bfloat16), high, low)


def unit_spread(x, means, start):
    rows, width = x.shape
    units = rows // UNIT
    half = pltpu.VMEM((units, width, width), jnp.bfloat16)
    return pl.pallas_call(
        spread_kernel,
        grid=(units,),
        in_specs=[
            pl.BlockSpec((UNIT, width), lambda u: (u, 0)),
            pl.BlockSpec((1, 1, width), lambda u: (u, 0, 0)),
            pl.BlockSpec((DIRS, width), lambda u: (0, 0)),
        ],
        out_specs=vmem(3),
        out_shape=[half, half, pltpu.VMEM((units, DIRS, width), jnp.float32)],
        compiler_params=pltpu.CompilerParams(vmem_limit_bytes=28 * MIB),
        name="unit_spread",
    )(x, means, start)


def flags(label_ref):
    units = label_ref.shape[0]
    same = [
        [jnp.where(label_ref[u] == label_ref[v], 1.0, 0.0) for v in range(units)] for u in range(units)
    ]
    return same, [same[u][0] for u in range(units)], [same[u][units - 1] for u in range(units)]


def merge_units(images, narrow, shift, same, out_ref, ends_ref):
    units = len(images)
    full = []
    for u in range(units):
        along = jnp.sum(narrow[u].astype(jnp.float32) * shift[u], axis=1, keepdims=True)
        full.append(images[u] + (UNIT * along) * shift[u])
    for u in range(units):
        total = full[u]
        for v in range(units):
            if v != u:
                total = total + full[v] * same[u][v]
        out_ref[u] = total
        if u == 0:
            ends_ref[:DIRS] = total
        if u == units - 1:
            ends_ref[DIRS:] = total


def first_kernel(label_ref, first_ref, last_ref, means_ref, start_ref, image_ref, out_ref, ends_ref, shift_ref):
    units = means_ref.shape[0]
    same, at_first, at_last = flags(label_ref)
    narrow = start_ref[...].astype(jnp.bfloat16)
    shift = []
    for u in range(units):
        total = first_ref[0:1] * at_first[u] + last_ref[0:1] * at_last[u]
        count = first_ref[1:2] * at_first[u] + last_ref[1:2] * at_last[u]
        for v in range(units):
            total = total + means_ref[v] * same[u][v]
            count = count + same[u][v]
        shift.append(means_ref[u] - total / count)
        shift_ref[u] = shift[u]
    merge_units([image_ref[u] for u in range(units)], [narrow] * units, shift, same, out_ref, ends_ref)


def vmem(count):
    return [pl.BlockSpec(memory_space=pltpu.VMEM)] * count


def smem(count):
    return [pl.BlockSpec(memory_space=pltpu.SMEM)] * count


def image_shapes(units, width):
    return [
        jax.ShapeDtypeStruct((units, DIRS, width), jnp.float32),
        jax.ShapeDtypeStruct((2 * DIRS, width), jnp.float32),
    ]


def first_images(labels, first, last_stats, means, start, images):
    units, _, width = means.shape
    return pl.pallas_call(
        first_kernel,
        in_specs=smem(1) + vmem(5),
        out_specs=vmem(3),
        out_shape=image_shapes(units, width) + [jax.ShapeDtypeStruct((units, 1, width), jnp.float32)],
        compiler_params=pltpu.CompilerParams(vmem_limit_bytes=4 * MIB),
        name="first_images",
    )(labels, first, last_stats, means, start, images)


def orthonormal(at_first, at_last, image_ref, first_ref, last_ref):
    units = image_ref.shape[0]
    size = units * DIRS
    first, last = first_ref[...], last_ref[...]
    images = jnp.concatenate(
        [image_ref[u] + first * at_first[u] + last * at_last[u] for u in range(units)], axis=0
    )
    gram = dot(images, images, ((1,), (1,)), HIGHEST)
    row = lax.broadcasted_iota(jnp.int32, (DIRS, size), 0)
    lane = lax.broadcasted_iota(jnp.int32, (DIRS, size), 1)
    inverse = []
    for u in range(units):
        left = gram[u * DIRS : (u + 1) * DIRS]
        right = (lane == row + u * DIRS).astype(jnp.float32)
        for k in range(DIRS - 1):
            c = u * DIRS + k
            factor = jnp.where(row[:, :1] > k, left[:, c : c + 1] / left[k : k + 1, c : c + 1], 0.0)
            right = right - factor * right[k : k + 1]
            left = left - factor * left[k : k + 1]
        diagonal = jnp.sum(jnp.where(lane == row + u * DIRS, left, 0.0), axis=1, keepdims=True)
        inverse.append(right / jnp.sqrt(diagonal))
    return dot(jnp.concatenate(inverse, axis=0), images, precision=HIGHEST)


def step_kernel(label_ref, image_ref, first_ref, last_ref, shift_ref, high_ref, low_ref, out_ref, ends_ref):
    units = image_ref.shape[0]
    same, at_first, at_last = flags(label_ref)
    basis = orthonormal(at_first, at_last, image_ref, first_ref, last_ref).astype(jnp.bfloat16)
    narrow = [basis[u * DIRS : (u + 1) * DIRS] for u in range(units)]
    images = [apply_unit(narrow[u], high_ref[u], low_ref[u]) for u in range(units)]
    merge_units(images, narrow, [shift_ref[u] for u in range(units)], same, out_ref, ends_ref)


def step(labels, images, first, last_image, shift, high, low):
    units, _, width = images.shape
    return pl.pallas_call(
        step_kernel,
        in_specs=smem(1) + vmem(6),
        out_specs=vmem(2),
        out_shape=image_shapes(units, width),
        compiler_params=pltpu.CompilerParams(vmem_limit_bytes=8 * MIB),
        name="step",
    )(labels, images, first, last_image, shift, high, low)


def last_kernel(label_ref, image_ref, first_ref, last_ref, mean_ref, shift_ref, x_ref, basis_ref, out_ref, narrow):
    units = image_ref.shape[0]
    u = pl.program_id(0)

    @pl.when(u == 0)
    def _():
        _, at_first, at_last = flags(label_ref)
        basis = orthonormal(at_first, at_last, image_ref, first_ref, last_ref)
        for v in range(units):
            basis_ref[v] = basis[v * DIRS : (v + 1) * DIRS]
            narrow[v] = basis[v * DIRS : (v + 1) * DIRS].astype(jnp.bfloat16)

    chosen = narrow[u]
    cluster_mean = mean_ref[u] - shift_ref[u]
    offset = jnp.sum(chosen.astype(jnp.float32) * cluster_mean, axis=1, keepdims=True)
    out_ref[...] = dot(chosen, x_ref[...], ((1,), (1,))) - offset


def last(labels, images, first, last_image, means, shift, x):
    rows, width = x.shape
    units = rows // UNIT
    whole = pl.BlockSpec((units, DIRS, width), lambda u: (0, 0, 0))
    one = pl.BlockSpec((DIRS, width), lambda u: (0, 0))
    line = pl.BlockSpec((units, 1, width), lambda u: (0, 0, 0))
    return pl.pallas_call(
        last_kernel,
        grid=(units,),
        in_specs=smem(1) + [whole, one, one, line, line, pl.BlockSpec((UNIT, width), lambda u: (u, 0))],
        out_specs=[whole, pl.BlockSpec((DIRS, UNIT), lambda u: (0, u))],
        out_shape=[
            jax.ShapeDtypeStruct((units, DIRS, width), jnp.float32),
            jax.ShapeDtypeStruct((DIRS, rows), jnp.float32),
        ],
        scratch_shapes=[pltpu.VMEM((units, DIRS, width), jnp.bfloat16)],
        compiler_params=pltpu.CompilerParams(vmem_limit_bytes=14 * MIB),
        name="last",
    )(labels, images, first, last_image, means, shift, x)


def per_device(n_dp, embeddings, cluster_ids, owner_table, start_basis):
    rows, width = embeddings.shape
    units = rows // UNIT
    chips = n_dp // 2
    me = lax.axis_index("dp")
    chip, core = me >> 1, me & 1
    even = core == 0
    labels = cluster_ids[::UNIT]

    near = (lambda p: p ^ 1, lambda p: (p + 1) % chips if p % 2 else (p - 1) % chips)
    far = (lambda p: p ^ 2, lambda p: (p + 2) % chips if p % 4 >= 2 else (p - 2) % chips)
    links = [
        [(2 * p + c, 2 * pairing[c](p) + c) for p in range(chips) for c in range(2)]
        for pairing in (near, far)
    ]
    upward = [(chip & 1) == core, ((chip >> 1) & 1) == core]
    mates = [(i, i ^ 1) for i in range(n_dp)]

    def halves(both):
        return both[:DIRS], both[DIRS:]

    def swap(both):
        return halves(lax.ppermute(both, "dp", mates))

    def chip_totals(own, mate, joins):
        head = jnp.where(even, own[0] + joins[0] * mate[0], mate[0] + joins[0] * own[0])
        tail = jnp.where(even, mate[1] + joins[1] * own[1], own[1] + joins[1] * mate[1])
        return head, tail

    def collect(left, right, own_side, mate, masks):
        mate_left, mate_right, at_head, at_tail = masks
        mate_side = swap(jnp.concatenate([left, right]))
        first = at_head * (left + mate_side[0]) + mate_left * mate[1]
        last_image = at_tail * (right + mate_side[1]) + mate_right * mate[0]
        return first, last_image

    means = unit_means(embeddings)
    row = lax.broadcasted_iota(jnp.int32, (DIRS, width), 0)

    def ends_stats(label):
        match = (labels == label).astype(jnp.float32)
        total = jnp.sum(match[:, None] * means.reshape(units, width), axis=0, keepdims=True)
        count = jnp.sum(match)
        return jnp.where(row == 0, total, jnp.where(row == 1, count, label.astype(jnp.float32)))

    own = jnp.concatenate([ends_stats(labels[0]), ends_stats(labels[-1])])
    mate = swap(own)
    own = halves(own)
    head, tail = own[0][2:3], own[1][2:3]
    mate_head, mate_tail = mate[0][2:3], mate[1][2:3]
    chip_head = jnp.where(even, head, mate_head)
    chip_tail = jnp.where(even, mate_tail, tail)

    def flag(value):
        return value.astype(jnp.float32)

    joins = flag(head == mate_head), flag(tail == mate_tail)
    masks = (
        flag(~even & (mate_tail == head)),
        flag(even & (mate_head == tail)),
        flag(head == chip_head),
        flag(tail == chip_tail),
    )
    totals = chip_totals(own, mate, joins)
    totals = jnp.where(row < 2, totals[0], chip_head), jnp.where(row < 2, totals[1], chip_tail)
    arrived = [
        lax.ppermute(jnp.where(up, totals[1], totals[0]), "dp", link) for link, up in zip(links, upward)
    ]
    high, low, raw = unit_spread(embeddings, means, start_basis)
    left = right = jnp.zeros((DIRS, width), jnp.float32)
    sides = []
    for got, up in zip(arrived, upward):
        from_left = flag(~up & (got[2:3] == chip_head))
        from_right = flag(up & (got[2:3] == chip_tail))
        sides.append((from_left, from_right))
        left = left + from_left * got
        right = right + from_right * got
    first_stats, last_stats = collect(left, right, own, mate, masks)

    def exchange(ends):
        mate, own = swap(ends), halves(ends)
        totals = chip_totals(own, mate, joins)
        left = right = jnp.zeros_like(own[0])
        for link, up, (from_left, from_right) in zip(links, upward, sides):
            got = lax.ppermute(jnp.where(up, totals[1], totals[0]), "dp", link)
            left = left + from_left * got
            right = right + from_right * got
        return collect(left, right, own, mate, masks)

    images, ends, shift = first_images(labels, first_stats, last_stats, means, start_basis, raw)
    for _ in range(ITERS - 1):
        images, ends = step(labels, images, *exchange(ends), shift, high, low)
    basis, projections = last(labels, images, *exchange(ends), means, shift, embeddings)

    starts = jnp.concatenate([first_stats[1, :1] == 0, labels[1:] != labels[:-1]])
    pick = (owner_table[:, None] == labels[None, :]) & starts[None, :]
    outgoing = jnp.einsum("ku,uid->kid", pick.astype(jnp.float32), basis, precision=HIGHEST)
    arrived = lax.all_to_all(outgoing, "dp", 0, 0, tiled=True)
    return jnp.sum(arrived, axis=0, keepdims=True), projections


def solution(mesh):
    in_specs = (P(("groups", "dp"), None), P(("groups", "dp")), P("groups"), P())
    out_specs = (P(("groups", "dp"), None, None), P(None, ("groups", "dp")))
    body = functools.partial(per_device, mesh.shape["dp"])
    return jax.shard_map(body, mesh=mesh, in_specs=in_specs, out_specs=out_specs, check_vma=False)
```

```python
import functools

import jax
import jax.numpy as jnp
from jax import lax
from jax.experimental import pallas as pl
from jax.experimental.pallas import tpu as pltpu
from jax.sharding import PartitionSpec as P

DIRS = 8
ITERS = 6
UNIT = 2048
HIGHEST = lax.Precision.HIGHEST
BLOCK = 256
CHUNKS = 16
PART = 1024
MIB = 1024 * 1024


def dot(a, b, contract=((1,), (0,)), precision=None):
    return lax.dot_general(
        a, b, (contract, ((), ())), precision=precision, preferred_element_type=jnp.float32
    )


def fetch(source, target, arrived, first, size):
    copies = []
    for i in range(target.shape[0] // size):
        part = source.at[pl.ds(first + i * size, size)]
        copies.append(pltpu.make_async_copy(part, target.at[pl.ds(i * size, size)], arrived.at[i]))
        copies[-1].start()
    return copies


def means_kernel(label_ref, source, means_ref, ends_ref, x_ref, arrived):
    units = means_ref.shape[0]
    size = x_ref.shape[0] // CHUNKS
    copies = fetch(source, x_ref, arrived, 0, size)
    for i in range(CHUNKS):
        copies[i].wait()
        part = jnp.sum(x_ref[i * size : (i + 1) * size].astype(jnp.float32), axis=0, keepdims=True)
        part = part * (1 / UNIT)
        u = i * size // UNIT
        means_ref[u] = part if i * size % UNIT == 0 else means_ref[u] + part
    same, _, _ = flags(label_ref)
    ends_ref[...] = jnp.zeros_like(ends_ref)
    for base, end in ((0, 0), (DIRS, units - 1)):
        total, count = jnp.zeros_like(part), jnp.zeros_like(part)
        for v in range(units):
            total = total + means_ref[v] * same[end][v]
            count = count + same[end][v]
        ends_ref[base : base + 1] = total
        ends_ref[base + 1 : base + 2] = count
        ends_ref[base + 2 : base + 3] = jnp.zeros_like(part) + label_ref[end].astype(jnp.float32)


def unit_means(labels, x):
    rows, width = x.shape
    units = rows // UNIT
    return pl.pallas_call(
        means_kernel,
        in_specs=smem(1) + [pl.BlockSpec(memory_space=pl.ANY)],
        out_specs=vmem(2),
        out_shape=[
            jax.ShapeDtypeStruct((units, 1, width), jnp.float32),
            jax.ShapeDtypeStruct((2 * DIRS, width), jnp.float32),
        ],
        scratch_shapes=[pltpu.VMEM(x.shape, x.dtype), pltpu.SemaphoreType.DMA((CHUNKS,))],
        compiler_params=pltpu.CompilerParams(vmem_limit_bytes=20 * MIB),
        name="unit_means",
    )(labels, x)


def apply_unit(narrow, spread_ref, u):
    return dot(narrow, spread_ref[0, u]) + dot(narrow, spread_ref[1, u])


def spread_kernel(x_ref, mean_ref, start_ref, spread_ref, image_ref, centered):
    u = pl.program_id(0)
    width = centered.shape[1]
    for a in range(0, UNIT, BLOCK):
        centered[a : a + BLOCK] = (x_ref[a : a + BLOCK].astype(jnp.float32) - mean_ref[0]).astype(jnp.bfloat16)
    for a in range(0, width, BLOCK):
        spread = dot(centered[:, a : a + BLOCK], centered[:, a:], ((0,), (0,)))
        high = spread.astype(jnp.bfloat16)
        low = (spread - high.astype(jnp.float32)).astype(jnp.bfloat16)
        for h, part in enumerate((high, low)):
            spread_ref[h, u, a : a + BLOCK, a:] = part
            if a + BLOCK < width:
                spread_ref[h, u, a + BLOCK :, a : a + BLOCK] = part[:, BLOCK:].T
    image_ref[u] = apply_unit(start_ref[...].astype(jnp.bfloat16), spread_ref, u)


def unit_spread(x, means, start):
    rows, width = x.shape
    units = rows // UNIT
    return pl.pallas_call(
        spread_kernel,
        grid=(units,),
        in_specs=[
            pl.BlockSpec((UNIT, width), lambda u: (u, 0)),
            pl.BlockSpec((1, 1, width), lambda u: (u, 0, 0)),
            pl.BlockSpec((DIRS, width), lambda u: (0, 0)),
        ],
        out_specs=vmem(2),
        out_shape=[
            pltpu.VMEM((2, units, width, width), jnp.bfloat16),
            jax.ShapeDtypeStruct((units, DIRS, width), jnp.float32),
        ],
        scratch_shapes=[pltpu.VMEM((UNIT, width), jnp.bfloat16)],
        compiler_params=pltpu.CompilerParams(vmem_limit_bytes=18 * MIB),
        name="unit_spread",
    )(x, means, start)


def flags(label_ref):
    units = label_ref.shape[0]
    same = [
        [jnp.where(label_ref[u] == label_ref[v], 1.0, 0.0) for v in range(units)] for u in range(units)
    ]
    return same, [same[u][0] for u in range(units)], [same[u][units - 1] for u in range(units)]


def merge_units(images, narrow, shift, same, out_ref, ends_ref):
    units = len(images)
    full = []
    for u in range(units):
        along = jnp.sum(narrow[u].astype(jnp.float32) * shift[u], axis=1, keepdims=True)
        full.append(images[u] + (UNIT * along) * shift[u])
    for u in range(units):
        total = full[u]
        for v in range(units):
            if v != u:
                total = total + full[v] * same[u][v]
        out_ref[u] = total
        if u == 0:
            ends_ref[:DIRS] = total
        if u == units - 1:
            ends_ref[DIRS:] = total


def first_kernel(label_ref, first_ref, last_ref, means_ref, start_ref, image_ref, out_ref, ends_ref, shift_ref):
    units = means_ref.shape[0]
    same, at_first, at_last = flags(label_ref)
    narrow = start_ref[...].astype(jnp.bfloat16)
    shift = []
    for u in range(units):
        total = first_ref[0:1] * at_first[u] + last_ref[0:1] * at_last[u]
        count = first_ref[1:2] * at_first[u] + last_ref[1:2] * at_last[u]
        for v in range(units):
            total = total + means_ref[v] * same[u][v]
            count = count + same[u][v]
        shift.append(means_ref[u] - total / count)
        shift_ref[u] = shift[u]
    merge_units([image_ref[u] for u in range(units)], [narrow] * units, shift, same, out_ref, ends_ref)


def vmem(count):
    return [pl.BlockSpec(memory_space=pltpu.VMEM)] * count


def smem(count):
    return [pl.BlockSpec(memory_space=pltpu.SMEM)] * count


def image_shapes(units, width):
    return [
        jax.ShapeDtypeStruct((units, DIRS, width), jnp.float32),
        jax.ShapeDtypeStruct((2 * DIRS, width), jnp.float32),
    ]


def first_images(labels, first, last_stats, means, start, images):
    units, _, width = means.shape
    return pl.pallas_call(
        first_kernel,
        in_specs=smem(1) + vmem(5),
        out_specs=vmem(3),
        out_shape=image_shapes(units, width) + [jax.ShapeDtypeStruct((units, 1, width), jnp.float32)],
        compiler_params=pltpu.CompilerParams(vmem_limit_bytes=4 * MIB),
        name="first_images",
    )(labels, first, last_stats, means, start, images)


def orthonormal(at_first, at_last, image_ref, first_ref, last_ref):
    units = image_ref.shape[0]
    size = units * DIRS
    first, last = first_ref[...], last_ref[...]
    images = jnp.concatenate(
        [image_ref[u] + first * at_first[u] + last * at_last[u] for u in range(units)], axis=0
    )
    gram = dot(images, images, ((1,), (1,)), HIGHEST)
    row = lax.broadcasted_iota(jnp.int32, (DIRS, size), 0)
    lane = lax.broadcasted_iota(jnp.int32, (DIRS, size), 1)
    inverse = []
    for u in range(units):
        left = gram[u * DIRS : (u + 1) * DIRS]
        right = (lane == row + u * DIRS).astype(jnp.float32)
        for k in range(DIRS - 1):
            c = u * DIRS + k
            factor = jnp.where(row[:, :1] > k, left[:, c : c + 1] / left[k : k + 1, c : c + 1], 0.0)
            right = right - factor * right[k : k + 1]
            left = left - factor * left[k : k + 1]
        diagonal = jnp.sum(jnp.where(lane == row + u * DIRS, left, 0.0), axis=1, keepdims=True)
        inverse.append(right / jnp.sqrt(diagonal))
    return dot(jnp.concatenate(inverse, axis=0), images, precision=HIGHEST)


def step_kernel(label_ref, image_ref, first_ref, last_ref, shift_ref, spread_ref, out_ref, ends_ref):
    units = image_ref.shape[0]
    same, at_first, at_last = flags(label_ref)
    basis = orthonormal(at_first, at_last, image_ref, first_ref, last_ref).astype(jnp.bfloat16)
    narrow = [basis[u * DIRS : (u + 1) * DIRS] for u in range(units)]
    images = [apply_unit(narrow[u], spread_ref, u) for u in range(units)]
    merge_units(images, narrow, [shift_ref[u] for u in range(units)], same, out_ref, ends_ref)


def route_kernel(owner_ref, me_ref, label_ref, *refs):
    *refs, kept_ref, sent_ref = refs
    step_kernel(label_ref, *refs)
    images = [refs[-2][u] for u in range(refs[-2].shape[0])]
    core = me_ref[0] & 1
    for j in range(kept_ref.shape[0]):
        for ref, bit in ((kept_ref, core), (sent_ref, 1 - core)):
            owner = owner_ref[2 * j + bit]
            total = jnp.zeros_like(images[0])
            for u, image in enumerate(images):
                chosen = label_ref[u] == owner
                if u > 0:
                    chosen = chosen & (label_ref[u] != label_ref[u - 1])
                total = total + image * jnp.where(chosen, 1.0, 0.0)
            ref[j] = total


def step(labels, images, first, last_image, shift, spread):
    units, _, width = images.shape
    return pl.pallas_call(
        step_kernel,
        in_specs=smem(1) + vmem(5),
        out_specs=vmem(2),
        out_shape=image_shapes(units, width),
        compiler_params=pltpu.CompilerParams(vmem_limit_bytes=8 * MIB),
        name="step",
    )(labels, images, first, last_image, shift, spread)


def step_and_route(owners, me, labels, images, first, last_image, shift, spread):
    units, _, width = images.shape
    tiles = jax.ShapeDtypeStruct((owners.shape[0] // 2, DIRS, width), jnp.float32)
    return pl.pallas_call(
        route_kernel,
        in_specs=smem(3) + vmem(5),
        out_specs=vmem(4),
        out_shape=image_shapes(units, width) + [tiles, tiles],
        compiler_params=pltpu.CompilerParams(vmem_limit_bytes=8 * MIB),
        name="step_and_route",
    )(owners, me.reshape(1), labels, images, first, last_image, shift, spread)


def project_half(first, narrow, mean_ref, shift_ref, x_ref, copies, out_ref):
    size = x_ref.shape[0] // len(copies)
    for i, copy in enumerate(copies):
        u = first + i * size // UNIT
        chosen = narrow[u * DIRS : (u + 1) * DIRS]
        mean = mean_ref[u] - shift_ref[u]
        offset = jnp.sum(chosen.astype(jnp.float32) * mean, axis=1, keepdims=True)
        copy.wait()
        rows = x_ref[i * size : (i + 1) * size]
        at = first * UNIT + i * size
        out_ref[:, at : at + size] = dot(chosen, rows, ((1,), (1,))) - offset


def early_kernel(
    label_ref, image_ref, first_ref, last_ref, mean_ref, shift_ref, source, narrow_ref, out_ref, x_ref, arrived
):
    copies = fetch(source, x_ref, arrived, 0, PART)
    _, at_first, at_last = flags(label_ref)
    narrow = orthonormal(at_first, at_last, image_ref, first_ref, last_ref).astype(jnp.bfloat16)
    narrow_ref[...] = narrow
    project_half(0, narrow, mean_ref, shift_ref, x_ref, copies, out_ref)


def late_kernel(narrow_ref, mean_ref, shift_ref, half_ref, source, out_ref, x_ref, arrived):
    first = mean_ref.shape[0] // 2
    copies = fetch(source, x_ref, arrived, first * UNIT, PART)
    out_ref[:, : half_ref.shape[1]] = half_ref[...]
    project_half(first, narrow_ref[...], mean_ref, shift_ref, x_ref, copies, out_ref)


def half_scratch(x):
    rows, width = x.shape
    return [
        pltpu.VMEM((rows // 2, width), x.dtype),
        pltpu.SemaphoreType.DMA((rows // 2 // PART,)),
    ]


def half_cost(rows, width):
    return pl.CostEstimate(flops=rows * width * 256, bytes_accessed=rows * width, transcendentals=0)


def project_early(labels, images, first, last_image, means, shift, x):
    rows, width = x.shape
    units = rows // UNIT
    return pl.pallas_call(
        early_kernel,
        in_specs=smem(1) + vmem(5) + [pl.BlockSpec(memory_space=pl.ANY)],
        out_specs=vmem(2),
        scratch_shapes=half_scratch(x),
        out_shape=[
            jax.ShapeDtypeStruct((units * DIRS, width), jnp.bfloat16),
            jax.ShapeDtypeStruct((DIRS, units // 2 * UNIT), jnp.float32),
        ],
        compiler_params=pltpu.CompilerParams(vmem_limit_bytes=12 * MIB),
        cost_estimate=half_cost(rows, width),
        name="project_early",
    )(labels, images, first, last_image, means, shift, x)


def project_late(narrow, means, shift, half, x):
    rows, width = x.shape
    return pl.pallas_call(
        late_kernel,
        in_specs=vmem(4) + [pl.BlockSpec(memory_space=pl.ANY)],
        out_specs=vmem(1)[0],
        scratch_shapes=half_scratch(x),
        out_shape=jax.ShapeDtypeStruct((DIRS, rows), jnp.float32),
        compiler_params=pltpu.CompilerParams(vmem_limit_bytes=12 * MIB),
        cost_estimate=half_cost(rows, width),
        name="project_late",
    )(narrow, means, shift, half, x)


def finish_kernel(kept_ref, got_ref, out_ref):
    out_ref[0] = orthonormal([1.0], [0.0], kept_ref, got_ref.at[0], got_ref.at[0])


def finish(kept, got):
    return pl.pallas_call(
        finish_kernel,
        in_specs=vmem(2),
        out_specs=vmem(1)[0],
        out_shape=jax.ShapeDtypeStruct(kept.shape, jnp.float32),
        compiler_params=pltpu.CompilerParams(vmem_limit_bytes=4 * MIB),
        name="finish",
    )(kept, got)


def per_device(n_dp, embeddings, cluster_ids, owner_table, start_basis):
    rows, width = embeddings.shape
    units = rows // UNIT
    chips = n_dp // 2
    me = lax.axis_index("dp")
    chip, core = me >> 1, me & 1
    even = core == 0
    labels = cluster_ids[::UNIT]

    near = (lambda p: p ^ 1, lambda p: (p + 1) % chips if p % 2 else (p - 1) % chips)
    far = (lambda p: p ^ 2, lambda p: (p + 2) % chips if p % 4 >= 2 else (p - 2) % chips)
    links = [
        [(2 * p + c, 2 * pairing[c](p) + c) for p in range(chips) for c in range(2)]
        for pairing in (near, far)
    ]
    upward = [(chip & 1) == core, ((chip >> 1) & 1) == core]
    mates = [(i, i ^ 1) for i in range(n_dp)]

    def halves(both):
        return both[:DIRS], both[DIRS:]

    def swap(both):
        return halves(lax.ppermute(both, "dp", mates))

    def chip_totals(own, mate, joins):
        head = jnp.where(even, own[0] + joins[0] * mate[0], mate[0] + joins[0] * own[0])
        tail = jnp.where(even, mate[1] + joins[1] * own[1], own[1] + joins[1] * mate[1])
        return head, tail

    def collect(left, right, own_side, mate, masks):
        mate_left, mate_right, at_head, at_tail = masks
        mate_side = swap(jnp.concatenate([left, right]))
        first = at_head * (left + mate_side[0]) + mate_left * mate[1]
        last_image = at_tail * (right + mate_side[1]) + mate_right * mate[0]
        return first, last_image

    embeddings = pltpu.with_memory_space_constraint(embeddings, pltpu.HBM)
    means, own = unit_means(labels, embeddings)
    row = lax.broadcasted_iota(jnp.int32, (DIRS, width), 0)
    mate = swap(own)
    own = halves(own)
    head, tail = own[0][2:3], own[1][2:3]
    mate_head, mate_tail = mate[0][2:3], mate[1][2:3]
    chip_head = jnp.where(even, head, mate_head)
    chip_tail = jnp.where(even, mate_tail, tail)

    def flag(value):
        return value.astype(jnp.float32)

    joins = flag(head == mate_head), flag(tail == mate_tail)
    masks = (
        flag(~even & (mate_tail == head)),
        flag(even & (mate_head == tail)),
        flag(head == chip_head),
        flag(tail == chip_tail),
    )
    totals = chip_totals(own, mate, joins)
    totals = jnp.where(row < 2, totals[0], chip_head), jnp.where(row < 2, totals[1], chip_tail)
    arrived = [
        lax.ppermute(jnp.where(up, totals[1], totals[0]), "dp", link) for link, up in zip(links, upward)
    ]
    spread, raw = unit_spread(embeddings, means, start_basis)
    raw, *arrived = lax.optimization_barrier((raw, *arrived))
    left = right = jnp.zeros((DIRS, width), jnp.float32)
    sides = []
    for got, up in zip(arrived, upward):
        from_left = flag(~up & (got[2:3] == chip_head))
        from_right = flag(up & (got[2:3] == chip_tail))
        sides.append((from_left, from_right))
        left = left + from_left * got
        right = right + from_right * got
    first_stats, last_stats = collect(left, right, own, mate, masks)

    def exchange(ends):
        mate, own = swap(ends), halves(ends)
        totals = chip_totals(own, mate, joins)
        left = right = jnp.zeros_like(own[0])
        for link, up, (from_left, from_right) in zip(links, upward, sides):
            got = lax.ppermute(jnp.where(up, totals[1], totals[0]), "dp", link)
            left = left + from_left * got
            right = right + from_right * got
        return collect(left, right, own, mate, masks)

    def halve(tiles, bit):
        low, high = tiles[0::2], tiles[1::2]
        set_here = (me & bit) != 0
        return jnp.where(set_here, high, low), jnp.where(set_here, low, high)

    def route(sent, bit):
        return lax.ppermute(sent, "dp", [(i, i ^ bit) for i in range(n_dp)])

    def split(tiles, bit):
        kept, sent = halve(tiles, bit)
        return kept + route(sent, bit)

    images, ends, shift = first_images(labels, first_stats, last_stats, means, start_basis, raw)
    for _ in range(ITERS - 2):
        images, ends = step(labels, images, *exchange(ends), shift, spread)

    images, ends, kept, sent = step_and_route(
        owner_table, me, labels, images, *exchange(ends), shift, spread
    )
    kept = kept + route(sent, 1)
    bit = 2
    while 2 * bit < n_dp:
        kept = split(kept, bit)
        bit *= 2
    kept, sent = halve(kept, bit)
    got = route(sent, bit)
    narrow, half = project_early(labels, images, *exchange(ends), means, shift, embeddings)
    projections = project_late(narrow, means, shift, half, embeddings)
    return finish(kept, got), projections


def solution(mesh):
    in_specs = (P(("groups", "dp"), None), P(("groups", "dp")), P("groups"), P())
    out_specs = (P(("groups", "dp"), None, None), P(None, ("groups", "dp")))
    body = functools.partial(per_device, mesh.shape["dp"])
    return jax.shard_map(body, mesh=mesh, in_specs=in_specs, out_specs=out_specs, check_vma=False)
```

```python
import functools

import jax
import jax.numpy as jnp
from jax import lax
from jax.experimental import pallas as pl
from jax.experimental.pallas import tpu as pltpu
from jax.sharding import PartitionSpec as P

DIRS = 8
ITERS = 6
UNIT = 2048
HIGHEST = lax.Precision.HIGHEST
BLOCK = 256
CHUNKS = 16
PART = 1024
MIB = 1024 * 1024


def dot(a, b, contract=((1,), (0,)), precision=None):
    return lax.dot_general(
        a, b, (contract, ((), ())), precision=precision, preferred_element_type=jnp.float32
    )


def fetch(source, target, arrived, first, size):
    copies = []
    for i in range(target.shape[0] // size):
        part = source.at[pl.ds(first + i * size, size)]
        copies.append(pltpu.make_async_copy(part, target.at[pl.ds(i * size, size)], arrived.at[i]))
        copies[-1].start()
    return copies


def means_kernel(label_ref, source, means_ref, ends_ref, x_ref, arrived):
    units = means_ref.shape[0]
    size = x_ref.shape[0] // CHUNKS
    copies = fetch(source, x_ref, arrived, 0, size)
    for i in range(CHUNKS):
        copies[i].wait()
        part = jnp.sum(x_ref[i * size : (i + 1) * size].astype(jnp.float32), axis=0, keepdims=True)
        part = part * (1 / UNIT)
        u = i * size // UNIT
        means_ref[u] = part if i * size % UNIT == 0 else means_ref[u] + part
    same, _, _ = flags(label_ref)
    ends_ref[...] = jnp.zeros_like(ends_ref)
    for base, end in ((0, 0), (DIRS, units - 1)):
        total, count = jnp.zeros_like(part), jnp.zeros_like(part)
        for v in range(units):
            total = total + means_ref[v] * same[end][v]
            count = count + same[end][v]
        ends_ref[base : base + 1] = total
        ends_ref[base + 1 : base + 2] = count
        ends_ref[base + 2 : base + 3] = jnp.zeros_like(part) + label_ref[end].astype(jnp.float32)


def unit_means(labels, x):
    rows, width = x.shape
    units = rows // UNIT
    return pl.pallas_call(
        means_kernel,
        in_specs=smem(1) + [pl.BlockSpec(memory_space=pl.ANY)],
        out_specs=vmem(2),
        out_shape=[
            jax.ShapeDtypeStruct((units, 1, width), jnp.float32),
            jax.ShapeDtypeStruct((2 * DIRS, width), jnp.float32),
        ],
        scratch_shapes=[pltpu.VMEM(x.shape, x.dtype), pltpu.SemaphoreType.DMA((CHUNKS,))],
        compiler_params=pltpu.CompilerParams(vmem_limit_bytes=20 * MIB),
        name="unit_means",
    )(labels, x)


def apply_unit(narrow, spread_ref, u):
    return dot(narrow, spread_ref[0, u]) + dot(narrow, spread_ref[1, u])


def spread_kernel(x_ref, mean_ref, start_ref, spread_ref, image_ref, centered):
    u = pl.program_id(0)
    width = centered.shape[1]
    for a in range(0, UNIT, BLOCK):
        centered[a : a + BLOCK] = (x_ref[a : a + BLOCK].astype(jnp.float32) - mean_ref[0]).astype(jnp.bfloat16)
    for a in range(0, width, BLOCK):
        spread = dot(centered[:, a : a + BLOCK], centered[:, a:], ((0,), (0,)))
        high = spread.astype(jnp.bfloat16)
        low = (spread - high.astype(jnp.float32)).astype(jnp.bfloat16)
        for h, part in enumerate((high, low)):
            spread_ref[h, u, a : a + BLOCK, a:] = part
            if a + BLOCK < width:
                spread_ref[h, u, a + BLOCK :, a : a + BLOCK] = part[:, BLOCK:].T
    image_ref[u] = apply_unit(start_ref[...].astype(jnp.bfloat16), spread_ref, u)


def unit_spread(x, means, start):
    rows, width = x.shape
    units = rows // UNIT
    return pl.pallas_call(
        spread_kernel,
        grid=(units,),
        in_specs=[
            pl.BlockSpec((UNIT, width), lambda u: (u, 0)),
            pl.BlockSpec((1, 1, width), lambda u: (u, 0, 0)),
            pl.BlockSpec((DIRS, width), lambda u: (0, 0)),
        ],
        out_specs=vmem(2),
        out_shape=[
            pltpu.VMEM((2, units, width, width), jnp.bfloat16),
            jax.ShapeDtypeStruct((units, DIRS, width), jnp.float32),
        ],
        scratch_shapes=[pltpu.VMEM((UNIT, width), jnp.bfloat16)],
        compiler_params=pltpu.CompilerParams(vmem_limit_bytes=18 * MIB),
        name="unit_spread",
    )(x, means, start)


def flags(label_ref):
    units = label_ref.shape[0]
    same = [
        [jnp.where(label_ref[u] == label_ref[v], 1.0, 0.0) for v in range(units)] for u in range(units)
    ]
    return same, [same[u][0] for u in range(units)], [same[u][units - 1] for u in range(units)]


def merge_units(images, narrow, shift, same, out_ref, ends_ref):
    units = len(images)
    full = []
    for u in range(units):
        along = jnp.sum(narrow[u].astype(jnp.float32) * shift[u], axis=1, keepdims=True)
        full.append(images[u] + (UNIT * along) * shift[u])
    for u in range(units):
        total = full[u]
        for v in range(units):
            if v != u:
                total = total + full[v] * same[u][v]
        out_ref[u] = total
        if u == 0:
            ends_ref[:DIRS] = total
        if u == units - 1:
            ends_ref[DIRS : 2 * DIRS] = total


def first_kernel(label_ref, first_ref, last_ref, means_ref, start_ref, image_ref, out_ref, ends_ref, shift_ref):
    units = means_ref.shape[0]
    same, at_first, at_last = flags(label_ref)
    narrow = start_ref[...].astype(jnp.bfloat16)
    shift = []
    for u in range(units):
        total = first_ref[0:1] * at_first[u] + last_ref[0:1] * at_last[u]
        count = first_ref[1:2] * at_first[u] + last_ref[1:2] * at_last[u]
        for v in range(units):
            total = total + means_ref[v] * same[u][v]
            count = count + same[u][v]
        shift.append(means_ref[u] - total / count)
        shift_ref[u] = shift[u]
    merge_units([image_ref[u] for u in range(units)], [narrow] * units, shift, same, out_ref, ends_ref)


def vmem(count):
    return [pl.BlockSpec(memory_space=pltpu.VMEM)] * count


def smem(count):
    return [pl.BlockSpec(memory_space=pltpu.SMEM)] * count


def image_shapes(units, width):
    return [
        jax.ShapeDtypeStruct((units, DIRS, width), jnp.float32),
        jax.ShapeDtypeStruct((2 * DIRS, width), jnp.float32),
    ]


def first_images(labels, first, last_stats, means, start, images):
    units, _, width = means.shape
    return pl.pallas_call(
        first_kernel,
        in_specs=smem(1) + vmem(5),
        out_specs=vmem(3),
        out_shape=image_shapes(units, width) + [jax.ShapeDtypeStruct((units, 1, width), jnp.float32)],
        compiler_params=pltpu.CompilerParams(vmem_limit_bytes=4 * MIB),
        name="first_images",
    )(labels, first, last_stats, means, start, images)


def inverse_factor(images, row, lane):
    shape = row.shape
    columns = [
        jnp.broadcast_to(jnp.sum(images * images[j : j + 1], axis=1, keepdims=True), shape)
        for j in range(DIRS)
    ]
    inverse = (lane == row).astype(jnp.float32)
    scale = jnp.zeros(shape, jnp.float32)
    for k in range(DIRS):
        pivot = columns[k][k : k + 1]
        scale = jnp.where(row == k, lax.rsqrt(pivot), scale)
        factor = jnp.where(row > k, columns[k] * (1.0 / pivot), 0.0)
        inverse = inverse - factor * inverse[k : k + 1]
        for j in range(k + 1, DIRS):
            columns[j] = columns[j] - factor * columns[j][k : k + 1]
    return inverse * scale


def orthonormal(at_first, at_last, image_ref, first_ref, last_ref):
    units = image_ref.shape[0]
    first, last = first_ref[...], last_ref[...]
    images = [image_ref[u] + first * at_first[u] + last * at_last[u] for u in range(units)]
    row = lax.broadcasted_iota(jnp.int32, (DIRS, units * DIRS), 0)
    lane = lax.broadcasted_iota(jnp.int32, (DIRS, units * DIRS), 1)
    inverse = [inverse_factor(images[u], row, lane - u * DIRS) for u in range(units)]
    return dot(jnp.concatenate(inverse, axis=0), jnp.concatenate(images, axis=0), precision=HIGHEST)


def step_kernel(label_ref, image_ref, first_ref, last_ref, shift_ref, spread_ref, out_ref, ends_ref):
    units = image_ref.shape[0]
    same, at_first, at_last = flags(label_ref)
    basis = orthonormal(at_first, at_last, image_ref, first_ref, last_ref).astype(jnp.bfloat16)
    narrow = [basis[u * DIRS : (u + 1) * DIRS] for u in range(units)]
    images = [apply_unit(narrow[u], spread_ref, u) for u in range(units)]
    merge_units(images, narrow, [shift_ref[u] for u in range(units)], same, out_ref, ends_ref)


def route_kernel(owner_ref, me_ref, label_ref, *refs):
    *refs, ends_ref, kept_ref = refs
    step_kernel(label_ref, *refs, ends_ref)
    images = [refs[-1][u] for u in range(refs[-1].shape[0])]
    core = me_ref[0] & 1
    count = kept_ref.shape[0] // DIRS
    for j in range(count):
        for ref, first, bit in ((kept_ref, 0, core), (ends_ref, 2 * DIRS, 1 - core)):
            owner = owner_ref[2 * j + bit]
            total = jnp.zeros_like(images[0])
            for u, image in enumerate(images):
                chosen = label_ref[u] == owner
                if u > 0:
                    chosen = chosen & (label_ref[u] != label_ref[u - 1])
                total = total + image * jnp.where(chosen, 1.0, 0.0)
            ref[first + j * DIRS : first + (j + 1) * DIRS] = total


def step(labels, images, first, last_image, shift, spread):
    units, _, width = images.shape
    return pl.pallas_call(
        step_kernel,
        in_specs=smem(1) + vmem(5),
        out_specs=vmem(2),
        out_shape=image_shapes(units, width),
        compiler_params=pltpu.CompilerParams(vmem_limit_bytes=8 * MIB),
        name="step",
    )(labels, images, first, last_image, shift, spread)


def step_and_route(owners, me, labels, images, first, last_image, shift, spread):
    units, _, width = images.shape
    tiles = owners.shape[0] // 2 * DIRS
    shapes = image_shapes(units, width)
    shapes[1] = jax.ShapeDtypeStruct((2 * DIRS + tiles, width), jnp.float32)
    shapes.append(jax.ShapeDtypeStruct((tiles, width), jnp.float32))
    return pl.pallas_call(
        route_kernel,
        in_specs=smem(3) + vmem(5),
        out_specs=vmem(3),
        out_shape=shapes,
        compiler_params=pltpu.CompilerParams(vmem_limit_bytes=8 * MIB),
        name="step_and_route",
    )(owners, me.reshape(1), labels, images, first, last_image, shift, spread)


def project_kernel(
    label_ref, image_ref, first_ref, last_ref, mean_ref, shift_ref, source, out_ref, x_ref, arrived
):
    copies = fetch(source, x_ref, arrived, 0, PART)
    _, at_first, at_last = flags(label_ref)
    narrow = orthonormal(at_first, at_last, image_ref, first_ref, last_ref).astype(jnp.bfloat16)
    for i, copy in enumerate(copies):
        u = i * PART // UNIT
        chosen = narrow[u * DIRS : (u + 1) * DIRS]
        mean = mean_ref[u] - shift_ref[u]
        offset = jnp.sum(chosen.astype(jnp.float32) * mean, axis=1, keepdims=True)
        copy.wait()
        rows = slice(i * PART, (i + 1) * PART)
        out_ref[:, rows] = dot(chosen, x_ref[rows], ((1,), (1,))) - offset


def project(labels, images, first, last_image, means, shift, x):
    rows, width = x.shape
    return pl.pallas_call(
        project_kernel,
        in_specs=smem(1) + vmem(5) + [pl.BlockSpec(memory_space=pl.ANY)],
        out_specs=vmem(1)[0],
        out_shape=jax.ShapeDtypeStruct((DIRS, rows), jnp.float32),
        scratch_shapes=[pltpu.VMEM(x.shape, x.dtype), pltpu.SemaphoreType.DMA((rows // PART,))],
        compiler_params=pltpu.CompilerParams(vmem_limit_bytes=24 * MIB),
        cost_estimate=pl.CostEstimate(
            flops=2 * rows * width * 256, bytes_accessed=2 * rows * width, transcendentals=0
        ),
        name="project",
    )(labels, images, first, last_image, means, shift, x)


def finish_kernel(kept_ref, got_ref, out_ref):
    out_ref[0] = orthonormal([1.0], [0.0], kept_ref, got_ref.at[0], got_ref.at[0])


def finish(kept, got):
    return pl.pallas_call(
        finish_kernel,
        in_specs=vmem(2),
        out_specs=vmem(1)[0],
        out_shape=jax.ShapeDtypeStruct(kept.shape, jnp.float32),
        compiler_params=pltpu.CompilerParams(vmem_limit_bytes=4 * MIB),
        name="finish",
    )(kept, got)


def per_device(n_dp, embeddings, cluster_ids, owner_table, start_basis):
    rows, width = embeddings.shape
    units = rows // UNIT
    chips = n_dp // 2
    me = lax.axis_index("dp")
    chip, core = me >> 1, me & 1
    even = core == 0
    labels = cluster_ids[::UNIT]

    near = (lambda p: p ^ 1, lambda p: (p + 1) % chips if p % 2 else (p - 1) % chips)
    far = (lambda p: p ^ 2, lambda p: (p + 2) % chips if p % 4 >= 2 else (p - 2) % chips)
    links = [
        [(2 * p + c, 2 * pairing[c](p) + c) for p in range(chips) for c in range(2)]
        for pairing in (near, far)
    ]
    upward = [(chip & 1) == core, ((chip >> 1) & 1) == core]
    mates = [(i, i ^ 1) for i in range(n_dp)]

    def halves(both):
        return both[:DIRS], both[DIRS:]

    def swap(both):
        return halves(lax.ppermute(both, "dp", mates))

    def chip_totals(own, mate, joins):
        head = jnp.where(even, own[0] + joins[0] * mate[0], mate[0] + joins[0] * own[0])
        tail = jnp.where(even, mate[1] + joins[1] * own[1], own[1] + joins[1] * mate[1])
        return head, tail

    def collect(left, right, own_side, mate, masks):
        mate_left, mate_right, at_head, at_tail = masks
        mate_side = swap(jnp.concatenate([left, right]))
        first = at_head * (left + mate_side[0]) + mate_left * mate[1]
        last_image = at_tail * (right + mate_side[1]) + mate_right * mate[0]
        return first, last_image

    embeddings = pltpu.with_memory_space_constraint(embeddings, pltpu.HBM)
    means, own = unit_means(labels, embeddings)
    row = lax.broadcasted_iota(jnp.int32, (DIRS, width), 0)
    mate = swap(own)
    own = halves(own)
    head, tail = own[0][2:3], own[1][2:3]
    mate_head, mate_tail = mate[0][2:3], mate[1][2:3]
    chip_head = jnp.where(even, head, mate_head)
    chip_tail = jnp.where(even, mate_tail, tail)

    def flag(value):
        return value.astype(jnp.float32)

    joins = flag(head == mate_head), flag(tail == mate_tail)
    masks = (
        flag(~even & (mate_tail == head)),
        flag(even & (mate_head == tail)),
        flag(head == chip_head),
        flag(tail == chip_tail),
    )
    totals = chip_totals(own, mate, joins)
    totals = jnp.where(row < 2, totals[0], chip_head), jnp.where(row < 2, totals[1], chip_tail)
    arrived = [
        lax.ppermute(jnp.where(up, totals[1], totals[0]), "dp", link) for link, up in zip(links, upward)
    ]
    spread, raw = unit_spread(embeddings, means, start_basis)
    raw, *arrived = lax.optimization_barrier((raw, *arrived))
    left = right = jnp.zeros((DIRS, width), jnp.float32)
    sides = []
    for got, up in zip(arrived, upward):
        from_left = flag(~up & (got[2:3] == chip_head))
        from_right = flag(up & (got[2:3] == chip_tail))
        sides.append((from_left, from_right))
        left = left + from_left * got
        right = right + from_right * got
    first_stats, last_stats = collect(left, right, own, mate, masks)

    def exchange(ends, mate=None, beside=lambda: ()):
        mate, own = mate or swap(ends), halves(ends)
        totals = chip_totals(own, mate, joins)
        arrived = [
            lax.ppermute(jnp.where(up, totals[1], totals[0]), "dp", link) for link, up in zip(links, upward)
        ]
        arrived, other = lax.optimization_barrier((arrived, beside()))
        left = right = jnp.zeros_like(own[0])
        for got, (from_left, from_right) in zip(arrived, sides):
            left = left + from_left * got
            right = right + from_right * got
        return *collect(left, right, own, mate, masks), other

    def halve(tiles, bit):
        low, high = tiles[0::2], tiles[1::2]
        set_here = (me & bit) != 0
        return jnp.where(set_here, high, low), jnp.where(set_here, low, high)

    def route(sent, bit):
        return lax.ppermute(sent, "dp", [(i, i ^ bit) for i in range(n_dp)])

    def split(tiles, bit):
        kept, sent = halve(tiles, bit)
        return kept + route(sent, bit)

    images, ends, shift = first_images(labels, first_stats, last_stats, means, start_basis, raw)
    for _ in range(ITERS - 2):
        images, ends = step(labels, images, *exchange(ends)[:2], shift, spread)

    images, ends, kept = step_and_route(
        owner_table, me, labels, images, *exchange(ends)[:2], shift, spread
    )
    got = lax.ppermute(ends, "dp", mates)
    kept = (kept + got[2 * DIRS :]).reshape(n_dp // 2, DIRS, width)
    kept, sent = halve(kept, 2)
    first, last_image, got = exchange(ends[: 2 * DIRS], halves(got[: 2 * DIRS]), lambda: route(sent, 2))
    kept = kept + got
    bit = 4
    while 2 * bit < n_dp:
        kept = split(kept, bit)
        bit *= 2
    kept, sent = halve(kept, bit)
    got = route(sent, bit)
    projections = project(labels, images, first, last_image, means, shift, embeddings)
    return finish(kept, got), projections


def solution(mesh):
    in_specs = (P(("groups", "dp"), None), P(("groups", "dp")), P("groups"), P())
    out_specs = (P(("groups", "dp"), None, None), P(None, ("groups", "dp")))
    body = functools.partial(per_device, mesh.shape["dp"])
    return jax.shard_map(body, mesh=mesh, in_specs=in_specs, out_specs=out_specs, check_vma=False)
```

```python
import functools

import jax
import jax.numpy as jnp
from jax import lax
from jax.experimental import pallas as pl
from jax.experimental.pallas import tpu as pltpu
from jax.sharding import PartitionSpec as P

DIRS = 8
ITERS = 6
UNIT = 2048
HIGHEST = lax.Precision.HIGHEST
BLOCK = 256
PART = 1024
MIB = 1024 * 1024


def dot(a, b, contract=((1,), (0,)), precision=None):
    return lax.dot_general(
        a, b, (contract, ((), ())), precision=precision, preferred_element_type=jnp.float32
    )


def fetch(source, target, arrived, first, size):
    copies = []
    for i in range(target.shape[0] // size):
        part = source.at[pl.ds(first + i * size, size)]
        copies.append(pltpu.make_async_copy(part, target.at[pl.ds(i * size, size)], arrived.at[i]))
        copies[-1].start()
    return copies


def apply_unit(narrow, spread_ref, u):
    return dot(narrow, spread_ref[0, u]) + dot(narrow, spread_ref[1, u])


def spread_kernel(label_ref, x_ref, start_ref, spread_ref, image_ref, mean_ref, ends_ref, centered):
    u = pl.program_id(0)
    width = centered.shape[1]
    ones = jnp.ones((DIRS, UNIT), jnp.bfloat16)
    mean = dot(ones, x_ref[...])[:1] * (1 / UNIT)
    mean_ref[u] = mean
    for a in range(0, UNIT, BLOCK):
        centered[a : a + BLOCK] = (x_ref[a : a + BLOCK].astype(jnp.float32) - mean).astype(jnp.bfloat16)
    for a in range(0, width, BLOCK):
        spread = dot(centered[:, a : a + BLOCK], centered[:, a:], ((0,), (0,)))
        high = spread.astype(jnp.bfloat16)
        low = (spread - high.astype(jnp.float32)).astype(jnp.bfloat16)
        for h, part in enumerate((high, low)):
            spread_ref[h, 0, a : a + BLOCK, a:] = part
            if a + BLOCK < width:
                spread_ref[h, 0, a + BLOCK :, a : a + BLOCK] = part[:, BLOCK:].T
    narrow = start_ref[...].astype(jnp.bfloat16)
    image_ref[u] = apply_unit(narrow, spread_ref, 0)

    @pl.when(u == pl.num_programs(0) - 1)
    def _():
        same, _, _ = flags(label_ref)
        units = image_ref.shape[0]
        for first, end in ((0, 0), (2 * DIRS, units - 1)):
            joined = join_units(end, same, narrow, image_ref, mean_ref)
            line = jnp.zeros_like(mean)
            parts = joined[0], joined[1], line + joined[2]
            put_block(ends_ref, first, parts, line + label_ref[end].astype(jnp.float32))


def join(narrow, a, b, mask):
    number = b[2] * mask
    total = a[2] + number
    share = number / jnp.maximum(total, 1.0)
    apart = b[1] - a[1]
    along = jnp.sum(narrow.astype(jnp.float32) * apart, axis=1, keepdims=True)
    images = a[0] + mask * b[0] + along * (UNIT * a[2] * share * apart)
    return images, a[1] + share * apart, total


def join_units(u, same, narrow, image_ref, mean_ref):
    joined = image_ref[u], mean_ref[u], jnp.float32(1.0)
    for v in range(image_ref.shape[0]):
        if v != u:
            joined = join(narrow, joined, (image_ref[v], mean_ref[v], jnp.float32(1.0)), same[u][v])
    return joined


def unit_spread(labels, x, start):
    rows, width = x.shape
    units = rows // UNIT
    return pl.pallas_call(
        spread_kernel,
        grid=(units,),
        in_specs=[
            *smem(1),
            pl.BlockSpec((UNIT, width), lambda u: (u, 0)),
            pl.BlockSpec((DIRS, width), lambda u: (0, 0)),
        ],
        out_specs=[pl.BlockSpec((2, 1, width, width), lambda u: (0, u, 0, 0)), *vmem(3)],
        out_shape=[
            pltpu.HBM((2, units, width, width), jnp.bfloat16),
            jax.ShapeDtypeStruct((units, DIRS, width), jnp.float32),
            jax.ShapeDtypeStruct((units, 1, width), jnp.float32),
            jax.ShapeDtypeStruct((4 * DIRS, width), jnp.float32),
        ],
        scratch_shapes=[pltpu.VMEM((UNIT, width), jnp.bfloat16)],
        compiler_params=pltpu.CompilerParams(vmem_limit_bytes=26 * MIB),
        name="unit_spread",
    )(labels, x, start)


def flags(label_ref):
    units = label_ref.shape[0]
    same = [
        [jnp.where(label_ref[u] == label_ref[v], 1.0, 0.0) for v in range(units)] for u in range(units)
    ]
    return same, [same[u][0] for u in range(units)], [same[u][units - 1] for u in range(units)]


def merge_units(images, narrow, shift, same, out_ref, ends_ref):
    units = len(images)
    full = []
    for u in range(units):
        along = jnp.sum(narrow[u].astype(jnp.float32) * shift[u], axis=1, keepdims=True)
        full.append(images[u] + (UNIT * along) * shift[u])
    for u in range(units):
        total = full[u]
        for v in range(units):
            if v != u:
                total = total + full[v] * same[u][v]
        out_ref[u] = total
        if u == 0:
            ends_ref[:DIRS] = total
        if u == units - 1:
            ends_ref[DIRS : 2 * DIRS] = total


def vmem(count):
    return [pl.BlockSpec(memory_space=pltpu.VMEM)] * count


def smem(count):
    return [pl.BlockSpec(memory_space=pltpu.SMEM)] * count


def image_shapes(units, width):
    return [
        jax.ShapeDtypeStruct((units, DIRS, width), jnp.float32),
        jax.ShapeDtypeStruct((2 * DIRS, width), jnp.float32),
    ]


def inverse_factor(images, row, lane):
    shape = row.shape
    columns = [
        jnp.broadcast_to(jnp.sum(images * images[j : j + 1], axis=1, keepdims=True), shape)
        for j in range(DIRS)
    ]
    inverse = (lane == row).astype(jnp.float32)
    scale = jnp.zeros(shape, jnp.float32)
    for k in range(DIRS):
        pivot = columns[k][k : k + 1]
        scale = jnp.where(row == k, lax.rsqrt(pivot), scale)
        factor = jnp.where(row > k, columns[k] * (1.0 / pivot), 0.0)
        inverse = inverse - factor * inverse[k : k + 1]
        for j in range(k + 1, DIRS):
            columns[j] = columns[j] - factor * columns[j][k : k + 1]
    return inverse * scale


def orthonormal(images):
    units = len(images)
    row = lax.broadcasted_iota(jnp.int32, (DIRS, units * DIRS), 0)
    lane = lax.broadcasted_iota(jnp.int32, (DIRS, units * DIRS), 1)
    inverse = [inverse_factor(images[u], row, lane - u * DIRS) for u in range(units)]
    return dot(jnp.concatenate(inverse, axis=0), jnp.concatenate(images, axis=0), precision=HIGHEST)


def whole_images(at_first, at_last, image_ref, first_ref, last_ref):
    first, last = first_ref[...], last_ref[...]
    return [
        image_ref[u] + first * at_first[u] + last * at_last[u] for u in range(image_ref.shape[0])
    ]


def multiply(totals, shift, same, spread_ref, out_ref, ends_ref, copies=()):
    units = len(totals)
    basis = orthonormal(totals).astype(jnp.bfloat16)
    narrow = [basis[u * DIRS : (u + 1) * DIRS] for u in range(units)]
    images = []
    for u in range(units):
        if copies:
            copies[u].wait()
        images.append(apply_unit(narrow[u], spread_ref, u))
    merge_units(images, narrow, shift, same, out_ref, ends_ref)


def block_at(ref, first):
    rest = first + DIRS
    return ref[first:rest], ref[rest : rest + 1], ref[rest + 1 : rest + 2], ref[rest + 2 : rest + 3]


def put_block(ref, first, parts, label):
    rest = first + DIRS
    ref[first:rest] = parts[0]
    for i, line in enumerate((parts[1], parts[2], label)):
        ref[rest + i : rest + i + 1] = line
    ref[rest + 3 : rest + DIRS] = jnp.zeros((DIRS - 3, ref.shape[1]), jnp.float32)


def upward(me):
    chip, core = me >> 1, me & 1
    return (chip & 1) == core, ((chip >> 1) & 1) == core


def flag(value):
    return jnp.where(value, 1.0, 0.0)


def chip_kernel(me_ref, own_ref, mate_ref, start_ref, near_ref, far_ref, mask_ref):
    even = (me_ref[0] & 1) == 0
    narrow = start_ref[...].astype(jnp.bfloat16)
    own = block_at(own_ref, 0), block_at(own_ref, 2 * DIRS)
    mate = block_at(mate_ref, 0), block_at(mate_ref, 2 * DIRS)
    head, tail, mate_head, mate_tail = own[0][3], own[1][3], mate[0][3], mate[1][3]
    chip_head = jnp.where(even, head, mate_head)
    chip_tail = jnp.where(even, mate_tail, tail)
    masks = [
        flag(head == mate_head),
        flag(tail == mate_tail),
        jnp.where(even, 0.0, flag(mate_tail == head)),
        jnp.where(even, flag(mate_head == tail), 0.0),
        flag(head == chip_head),
        flag(tail == chip_tail),
        chip_head,
        chip_tail,
    ]
    for i, line in enumerate(masks):
        mask_ref[i : i + 1] = line

    def order(a, b):
        return [jnp.where(even, x, y) for x, y in zip(a, b)], [jnp.where(even, y, x) for x, y in zip(a, b)]

    at_head = join(narrow, *order(own[0], mate[0]), masks[0])
    at_tail = join(narrow, *order(mate[1], own[1]), masks[1])
    for ref, up in zip((near_ref, far_ref), upward(me_ref[0])):
        parts = [jnp.where(up, x, y) for x, y in zip(at_tail, at_head)]
        put_block(ref, 0, parts, jnp.where(up, chip_tail, chip_head))


def join_chip(me, own, mate, start):
    width = own.shape[1]
    part = jax.ShapeDtypeStruct((2 * DIRS, width), jnp.float32)
    return pl.pallas_call(
        chip_kernel,
        in_specs=smem(1) + vmem(3),
        out_specs=vmem(3),
        out_shape=[part, part, jax.ShapeDtypeStruct((DIRS, width), jnp.float32)],
        compiler_params=pltpu.CompilerParams(vmem_limit_bytes=4 * MIB),
        name="join_chip",
    )(me, own, mate, start)


def sides_kernel(me_ref, near_ref, far_ref, mask_ref, start_ref, side_ref, from_ref):
    narrow = start_ref[...].astype(jnp.bfloat16)
    chip_head, chip_tail = mask_ref[6:7], mask_ref[7:8]
    line = jnp.zeros_like(chip_head)
    left = right = (jnp.zeros(start_ref.shape, jnp.float32), line, line)
    from_ref[...] = jnp.zeros_like(from_ref)
    for i, (ref, up) in enumerate(zip((near_ref, far_ref), upward(me_ref[0]))):
        got = block_at(ref, 0)
        from_left = jnp.where(up, 0.0, flag(got[3] == chip_head))
        from_right = jnp.where(up, flag(got[3] == chip_tail), 0.0)
        from_ref[2 * i : 2 * i + 1] = from_left
        from_ref[2 * i + 1 : 2 * i + 2] = from_right
        left = join(narrow, left, got, from_left)
        right = join(narrow, right, got, from_right)
    put_block(side_ref, 0, left, line)
    put_block(side_ref, 2 * DIRS, right, line)


def join_sides(me, near, far, masks, start):
    width = near.shape[1]
    return pl.pallas_call(
        sides_kernel,
        in_specs=smem(1) + vmem(4),
        out_specs=vmem(2),
        out_shape=[
            jax.ShapeDtypeStruct((4 * DIRS, width), jnp.float32),
            jax.ShapeDtypeStruct((DIRS, width), jnp.float32),
        ],
        compiler_params=pltpu.CompilerParams(vmem_limit_bytes=4 * MIB),
        name="join_sides",
    )(me, near, far, masks, start)


def first_kernel(
    label_ref, image_ref, mean_ref, mate_ref, side_ref, other_ref, mask_ref, start_ref, source,
    out_ref, ends_ref, shift_ref, spread_ref, arrived,
):
    units = image_ref.shape[0]
    copies = []
    for u in range(units):
        copies.append(pltpu.make_async_copy(source.at[:, u], spread_ref.at[:, u], arrived.at[u]))
        copies[u].start()
    same, at_first, at_last = flags(label_ref)
    narrow = start_ref[...].astype(jnp.bfloat16)
    outer = []
    for first, mate_first, row in ((0, 2 * DIRS, 0), (2 * DIRS, 0, 1)):
        side = join(narrow, block_at(side_ref, first), block_at(other_ref, first), 1.0)
        mask = mask_ref[4 + row : 5 + row]
        side = side[0] * mask, side[1], side[2] * mask
        outer.append(join(narrow, side, block_at(mate_ref, mate_first), mask_ref[2 + row : 3 + row]))
    totals, shift = [], []
    for u in range(units):
        joined = join_units(u, same, narrow, image_ref, mean_ref)
        joined = join(narrow, joined, outer[0], at_first[u])
        joined = join(narrow, joined, outer[1], at_last[u])
        totals.append(joined[0])
        shift.append(mean_ref[u] - joined[1])
        shift_ref[u] = shift[u]
    multiply(totals, shift, same, spread_ref, out_ref, ends_ref, copies)


def first_step(labels, images, means, mate, side, other, masks, start, spread):
    units, _, width = images.shape
    return pl.pallas_call(
        first_kernel,
        in_specs=smem(1) + vmem(7) + [pl.BlockSpec(memory_space=pl.ANY)],
        out_specs=vmem(4),
        out_shape=[
            *image_shapes(units, width),
            jax.ShapeDtypeStruct((units, 1, width), jnp.float32),
            pltpu.VMEM(spread.shape, spread.dtype),
        ],
        scratch_shapes=[pltpu.SemaphoreType.DMA((units,))],
        compiler_params=pltpu.CompilerParams(vmem_limit_bytes=8 * MIB),
        name="first_step",
    )(labels, images, means, mate, side, other, masks, start, spread)


def step_kernel(label_ref, image_ref, first_ref, last_ref, shift_ref, spread_ref, out_ref, ends_ref):
    same, at_first, at_last = flags(label_ref)
    totals = whole_images(at_first, at_last, image_ref, first_ref, last_ref)
    shift = [shift_ref[u] for u in range(image_ref.shape[0])]
    multiply(totals, shift, same, spread_ref, out_ref, ends_ref)


def route_kernel(owner_ref, me_ref, label_ref, *refs):
    *refs, ends_ref, kept_ref = refs
    step_kernel(label_ref, *refs, ends_ref)
    images = [refs[-1][u] for u in range(refs[-1].shape[0])]
    core = me_ref[0] & 1
    count = kept_ref.shape[0] // DIRS
    for j in range(count):
        for ref, first, bit in ((kept_ref, 0, core), (ends_ref, 2 * DIRS, 1 - core)):
            owner = owner_ref[2 * j + bit]
            total = jnp.zeros_like(images[0])
            for u, image in enumerate(images):
                chosen = label_ref[u] == owner
                if u > 0:
                    chosen = chosen & (label_ref[u] != label_ref[u - 1])
                total = total + image * jnp.where(chosen, 1.0, 0.0)
            ref[first + j * DIRS : first + (j + 1) * DIRS] = total


def step(labels, images, first, last_image, shift, spread):
    units, _, width = images.shape
    return pl.pallas_call(
        step_kernel,
        in_specs=smem(1) + vmem(5),
        out_specs=vmem(2),
        out_shape=image_shapes(units, width),
        compiler_params=pltpu.CompilerParams(vmem_limit_bytes=8 * MIB),
        name="step",
    )(labels, images, first, last_image, shift, spread)


def step_and_route(owners, me, labels, images, first, last_image, shift, spread):
    units, _, width = images.shape
    tiles = owners.shape[0] // 2 * DIRS
    shapes = image_shapes(units, width)
    shapes[1] = jax.ShapeDtypeStruct((2 * DIRS + tiles, width), jnp.float32)
    shapes.append(jax.ShapeDtypeStruct((tiles, width), jnp.float32))
    return pl.pallas_call(
        route_kernel,
        in_specs=smem(3) + vmem(5),
        out_specs=vmem(3),
        out_shape=shapes,
        compiler_params=pltpu.CompilerParams(vmem_limit_bytes=8 * MIB),
        name="step_and_route",
    )(owners, me, labels, images, first, last_image, shift, spread)


def project_kernel(
    label_ref, image_ref, first_ref, last_ref, mean_ref, shift_ref, source, out_ref, x_ref, arrived
):
    copies = fetch(source, x_ref, arrived, 0, PART)
    _, at_first, at_last = flags(label_ref)
    totals = whole_images(at_first, at_last, image_ref, first_ref, last_ref)
    narrow = orthonormal(totals).astype(jnp.bfloat16)
    for i, copy in enumerate(copies):
        u = i * PART // UNIT
        chosen = narrow[u * DIRS : (u + 1) * DIRS]
        mean = mean_ref[u] - shift_ref[u]
        offset = jnp.sum(chosen.astype(jnp.float32) * mean, axis=1, keepdims=True)
        copy.wait()
        rows = slice(i * PART, (i + 1) * PART)
        out_ref[:, rows] = dot(chosen, x_ref[rows], ((1,), (1,))) - offset


def project(labels, images, first, last_image, means, shift, x):
    rows, width = x.shape
    return pl.pallas_call(
        project_kernel,
        in_specs=smem(1) + vmem(5) + [pl.BlockSpec(memory_space=pl.ANY)],
        out_specs=vmem(1)[0],
        out_shape=jax.ShapeDtypeStruct((DIRS, rows), jnp.float32),
        scratch_shapes=[pltpu.VMEM(x.shape, x.dtype), pltpu.SemaphoreType.DMA((rows // PART,))],
        compiler_params=pltpu.CompilerParams(vmem_limit_bytes=24 * MIB),
        cost_estimate=pl.CostEstimate(
            flops=2 * rows * width * 256, bytes_accessed=2 * rows * width, transcendentals=0
        ),
        name="project",
    )(labels, images, first, last_image, means, shift, x)


def finish_kernel(kept_ref, got_ref, out_ref):
    out_ref[0] = orthonormal([kept_ref[0] + got_ref[0]])


def finish(kept, got):
    return pl.pallas_call(
        finish_kernel,
        in_specs=vmem(2),
        out_specs=vmem(1)[0],
        out_shape=jax.ShapeDtypeStruct(kept.shape, jnp.float32),
        compiler_params=pltpu.CompilerParams(vmem_limit_bytes=4 * MIB),
        name="finish",
    )(kept, got)


def per_device(n_dp, embeddings, cluster_ids, owner_table, start_basis):
    rows, width = embeddings.shape
    units = rows // UNIT
    chips = n_dp // 2
    me = lax.axis_index("dp")
    even = (me & 1) == 0
    labels = cluster_ids[::UNIT]

    near = (lambda p: p ^ 1, lambda p: (p + 1) % chips if p % 2 else (p - 1) % chips)
    far = (lambda p: p ^ 2, lambda p: (p + 2) % chips if p % 4 >= 2 else (p - 2) % chips)
    links = [
        [(2 * p + c, 2 * pairing[c](p) + c) for p in range(chips) for c in range(2)]
        for pairing in (near, far)
    ]
    mates = [(i, i ^ 1) for i in range(n_dp)]

    def halves(both):
        return both[:DIRS], both[DIRS:]

    def swap(both):
        return halves(lax.ppermute(both, "dp", mates))

    def chip_totals(own, mate, joins):
        head = jnp.where(even, own[0] + joins[0] * mate[0], mate[0] + joins[0] * own[0])
        tail = jnp.where(even, mate[1] + joins[1] * own[1], own[1] + joins[1] * mate[1])
        return head, tail

    def collect(left, right, own_side, mate, masks):
        mate_left, mate_right, at_head, at_tail = masks
        mate_side = swap(jnp.concatenate([left, right]))
        first = at_head * (left + mate_side[0]) + mate_left * mate[1]
        last_image = at_tail * (right + mate_side[1]) + mate_right * mate[0]
        return first, last_image

    embeddings = pltpu.with_memory_space_constraint(embeddings, pltpu.HBM)
    spread, raw, means, own = unit_spread(labels, embeddings, start_basis)

    place = me.reshape(1)
    mate = lax.ppermute(own, "dp", mates)
    near, far, masks = join_chip(place, own, mate, start_basis)
    near, far = (lax.ppermute(part, "dp", link) for part, link in zip((near, far), links))
    side, origins = join_sides(place, near, far, masks, start_basis)
    other = lax.ppermute(side, "dp", mates)
    images, ends, shift, spread = first_step(
        labels, raw, means, mate, side, other, masks, start_basis,
        pltpu.with_memory_space_constraint(spread, pltpu.HBM),
    )
    joins = masks[0:1], masks[1:2]
    masks = tuple(masks[i : i + 1] for i in range(2, 6))
    sides = [(origins[i : i + 1], origins[i + 1 : i + 2]) for i in (0, 2)]
    ups = upward(me)

    def exchange(ends, mate=None, beside=lambda: ()):
        mate, own = mate or swap(ends), halves(ends)
        totals = chip_totals(own, mate, joins)
        arrived = [
            lax.ppermute(jnp.where(up, totals[1], totals[0]), "dp", link) for link, up in zip(links, ups)
        ]
        arrived, other = lax.optimization_barrier((arrived, beside()))
        left = right = jnp.zeros_like(own[0])
        for got, (from_left, from_right) in zip(arrived, sides):
            left = left + from_left * got
            right = right + from_right * got
        return *collect(left, right, own, mate, masks), other

    def halve(tiles, bit):
        low, high = tiles[0::2], tiles[1::2]
        set_here = (me & bit) != 0
        return jnp.where(set_here, high, low), jnp.where(set_here, low, high)

    def route(sent, bit):
        return lax.ppermute(sent, "dp", [(i, i ^ bit) for i in range(n_dp)])

    def split(tiles, bit):
        kept, sent = halve(tiles, bit)
        return kept + route(sent, bit)

    for _ in range(ITERS - 3):
        images, ends = step(labels, images, *exchange(ends)[:2], shift, spread)

    images, ends, kept = step_and_route(
        owner_table, place, labels, images, *exchange(ends)[:2], shift, spread
    )
    got = lax.ppermute(ends, "dp", mates)
    kept = (kept + got[2 * DIRS :]).reshape(n_dp // 2, DIRS, width)
    kept, sent = halve(kept, 2)
    first, last_image, got = exchange(ends[: 2 * DIRS], halves(got[: 2 * DIRS]), lambda: route(sent, 2))
    kept = kept + got
    bit = 4
    while 2 * bit < n_dp:
        kept = split(kept, bit)
        bit *= 2
    kept, sent = halve(kept, bit)
    got = route(sent, bit)
    projections = project(labels, images, first, last_image, means, shift, embeddings)
    return finish(kept, got), projections


def solution(mesh):
    in_specs = (P(("groups", "dp"), None), P(("groups", "dp")), P("groups"), P())
    out_specs = (P(("groups", "dp"), None, None), P(None, ("groups", "dp")))
    body = functools.partial(per_device, mesh.shape["dp"])
    return jax.shard_map(body, mesh=mesh, in_specs=in_specs, out_specs=out_specs, check_vma=False)
```

```python
import functools

import jax
import jax.numpy as jnp
from jax import lax
from jax.experimental import pallas as pl
from jax.experimental.pallas import tpu as pltpu
from jax.sharding import PartitionSpec as P

DIRS = 8
ITERS = 6
UNIT = 2048
HIGHEST = lax.Precision.HIGHEST
BLOCK = 256
PART = 1024
MIB = 1024 * 1024


def dot(a, b, contract=((1,), (0,)), precision=None):
    return lax.dot_general(
        a, b, (contract, ((), ())), precision=precision, preferred_element_type=jnp.float32
    )


def fetch(source, target, arrived, first, size):
    copies = []
    for i in range(target.shape[0] // size):
        part = source.at[pl.ds(first + i * size, size)]
        copies.append(pltpu.make_async_copy(part, target.at[pl.ds(i * size, size)], arrived.at[i]))
        copies[-1].start()
    return copies


def apply_unit(narrow, spread_ref, u):
    return dot(narrow, spread_ref[0, u]) + dot(narrow, spread_ref[1, u])


def spread_kernel(_, label_ref, x_ref, start_ref, spread_ref, image_ref, mean_ref, ends_ref, centered):
    u = pl.program_id(0)
    width = centered.shape[1]
    ones = jnp.ones((DIRS, UNIT), jnp.bfloat16)
    mean = dot(ones, x_ref[...])[:1] * (1 / UNIT)
    mean_ref[u] = mean
    for a in range(0, UNIT, BLOCK):
        centered[a : a + BLOCK] = (x_ref[a : a + BLOCK].astype(jnp.float32) - mean).astype(jnp.bfloat16)
    for a in range(0, width, BLOCK):
        spread = dot(centered[:, a : a + BLOCK], centered[:, a:], ((0,), (0,)))
        high = spread.astype(jnp.bfloat16)
        low = (spread - high.astype(jnp.float32)).astype(jnp.bfloat16)
        for h, part in enumerate((high, low)):
            spread_ref[h, u, a : a + BLOCK, a:] = part
            if a + BLOCK < width:
                spread_ref[h, u, a + BLOCK :, a : a + BLOCK] = part[:, BLOCK:].T
    narrow = start_ref[...].astype(jnp.bfloat16)
    image_ref[u] = apply_unit(narrow, spread_ref, u)

    @pl.when(u == pl.num_programs(0) - 1)
    def _():
        same, _, _ = flags(label_ref)
        units = image_ref.shape[0]
        for first, end in ((0, 0), (2 * DIRS, units - 1)):
            joined = join_units(end, same, narrow, image_ref, mean_ref)
            line = jnp.zeros_like(mean)
            parts = joined[0], joined[1], line + joined[2]
            put_block(ends_ref, first, parts, line + label_ref[end].astype(jnp.float32))


def join(narrow, a, b, mask):
    number = b[2] * mask
    total = a[2] + number
    share = number / jnp.maximum(total, 1.0)
    apart = b[1] - a[1]
    along = jnp.sum(narrow.astype(jnp.float32) * apart, axis=1, keepdims=True)
    images = a[0] + mask * b[0] + along * (UNIT * a[2] * share * apart)
    return images, a[1] + share * apart, total


def join_units(u, same, narrow, image_ref, mean_ref):
    joined = image_ref[u], mean_ref[u], jnp.float32(1.0)
    for v in range(image_ref.shape[0]):
        if v != u:
            joined = join(narrow, joined, (image_ref[v], mean_ref[v], jnp.float32(1.0)), same[u][v])
    return joined


def unit_spread(me, labels, x, start):
    rows, width = x.shape
    units = rows // UNIT
    return pl.pallas_call(
        spread_kernel,
        grid=(units,),
        in_specs=[
            *smem(2),
            pl.BlockSpec((UNIT, width), lambda u: (u, 0)),
            pl.BlockSpec((DIRS, width), lambda u: (0, 0)),
        ],
        out_specs=vmem(4),
        out_shape=[
            pltpu.VMEM((2, units, width, width), jnp.bfloat16),
            jax.ShapeDtypeStruct((units, DIRS, width), jnp.float32),
            jax.ShapeDtypeStruct((units, 1, width), jnp.float32),
            jax.ShapeDtypeStruct((4 * DIRS, width), jnp.float32),
        ],
        scratch_shapes=[pltpu.VMEM((UNIT, width), jnp.bfloat16)],
        compiler_params=pltpu.CompilerParams(vmem_limit_bytes=18 * MIB),
        name="unit_spread",
    )(me, labels, x, start)


def flags(label_ref):
    units = label_ref.shape[0]
    same = [
        [jnp.where(label_ref[u] == label_ref[v], 1.0, 0.0) for v in range(units)] for u in range(units)
    ]
    return same, [same[u][0] for u in range(units)], [same[u][units - 1] for u in range(units)]


def merge_units(images, narrow, shift, same, out_ref, ends_ref):
    units = len(images)
    full = []
    for u in range(units):
        along = jnp.sum(narrow[u].astype(jnp.float32) * shift[u], axis=1, keepdims=True)
        full.append(images[u] + (UNIT * along) * shift[u])
    for u in range(units):
        total = full[u]
        for v in range(units):
            if v != u:
                total = total + full[v] * same[u][v]
        out_ref[u] = total
        if u == 0:
            ends_ref[:DIRS] = total
        if u == units - 1:
            ends_ref[DIRS : 2 * DIRS] = total


def vmem(count):
    return [pl.BlockSpec(memory_space=pltpu.VMEM)] * count


def smem(count):
    return [pl.BlockSpec(memory_space=pltpu.SMEM)] * count


def image_shapes(units, width):
    return [
        jax.ShapeDtypeStruct((units, DIRS, width), jnp.float32),
        jax.ShapeDtypeStruct((2 * DIRS, width), jnp.float32),
    ]


def inverse_factor(images, row, lane):
    shape = row.shape
    columns = [
        jnp.broadcast_to(jnp.sum(images * images[j : j + 1], axis=1, keepdims=True), shape)
        for j in range(DIRS)
    ]
    inverse = (lane == row).astype(jnp.float32)
    scale = jnp.zeros(shape, jnp.float32)
    for k in range(DIRS):
        pivot = columns[k][k : k + 1]
        scale = jnp.where(row == k, lax.rsqrt(pivot), scale)
        factor = jnp.where(row > k, columns[k] * (1.0 / pivot), 0.0)
        inverse = inverse - factor * inverse[k : k + 1]
        for j in range(k + 1, DIRS):
            columns[j] = columns[j] - factor * columns[j][k : k + 1]
    return inverse * scale


def orthonormal(images):
    units = len(images)
    row = lax.broadcasted_iota(jnp.int32, (DIRS, units * DIRS), 0)
    lane = lax.broadcasted_iota(jnp.int32, (DIRS, units * DIRS), 1)
    inverse = [inverse_factor(images[u], row, lane - u * DIRS) for u in range(units)]
    return dot(jnp.concatenate(inverse, axis=0), jnp.concatenate(images, axis=0), precision=HIGHEST)


def whole_images(at_first, at_last, image_ref, first_ref, last_ref):
    first, last = first_ref[...], last_ref[...]
    return [
        image_ref[u] + first * at_first[u] + last * at_last[u] for u in range(image_ref.shape[0])
    ]


def multiply(totals, shift, same, spread_ref, out_ref, ends_ref):
    units = len(totals)
    basis = orthonormal(totals).astype(jnp.bfloat16)
    narrow = [basis[u * DIRS : (u + 1) * DIRS] for u in range(units)]
    images = [apply_unit(narrow[u], spread_ref, u) for u in range(units)]
    merge_units(images, narrow, shift, same, out_ref, ends_ref)


def block_at(ref, first):
    rest = first + DIRS
    return ref[first:rest], ref[rest : rest + 1], ref[rest + 1 : rest + 2], ref[rest + 2 : rest + 3]


def put_block(ref, first, parts, label):
    rest = first + DIRS
    ref[first:rest] = parts[0]
    for i, line in enumerate((parts[1], parts[2], label)):
        ref[rest + i : rest + i + 1] = line
    ref[rest + 3 : rest + DIRS] = jnp.zeros((DIRS - 3, ref.shape[1]), jnp.float32)


def upward(me):
    chip, core = me >> 1, me & 1
    return (chip & 1) == core, ((chip >> 1) & 1) == core


def flag(value):
    return jnp.where(value, 1.0, 0.0)


def chip_kernel(me_ref, own_ref, mate_ref, start_ref, near_ref, far_ref, mask_ref):
    even = (me_ref[0] & 1) == 0
    narrow = start_ref[...].astype(jnp.bfloat16)
    own = block_at(own_ref, 0), block_at(own_ref, 2 * DIRS)
    mate = block_at(mate_ref, 0), block_at(mate_ref, 2 * DIRS)
    head, tail, mate_head, mate_tail = own[0][3], own[1][3], mate[0][3], mate[1][3]
    chip_head = jnp.where(even, head, mate_head)
    chip_tail = jnp.where(even, mate_tail, tail)
    masks = [
        flag(head == mate_head),
        flag(tail == mate_tail),
        jnp.where(even, 0.0, flag(mate_tail == head)),
        jnp.where(even, flag(mate_head == tail), 0.0),
        flag(head == chip_head),
        flag(tail == chip_tail),
        chip_head,
        chip_tail,
        *(jnp.where(value, 1.0, jnp.zeros_like(head)) for value in (even, *upward(me_ref[0]))),
    ]
    mask_ref[...] = jnp.zeros_like(mask_ref)
    for i, line in enumerate(masks):
        mask_ref[i : i + 1] = line

    def order(a, b):
        return [jnp.where(even, x, y) for x, y in zip(a, b)], [jnp.where(even, y, x) for x, y in zip(a, b)]

    at_head = join(narrow, *order(own[0], mate[0]), masks[0])
    at_tail = join(narrow, *order(mate[1], own[1]), masks[1])
    for ref, up in zip((near_ref, far_ref), upward(me_ref[0])):
        parts = [jnp.where(up, x, y) for x, y in zip(at_tail, at_head)]
        put_block(ref, 0, parts, jnp.where(up, chip_tail, chip_head))


def join_chip(me, own, mate, start):
    width = own.shape[1]
    part = jax.ShapeDtypeStruct((2 * DIRS, width), jnp.float32)
    return pl.pallas_call(
        chip_kernel,
        in_specs=smem(1) + vmem(3),
        out_specs=vmem(3),
        out_shape=[part, part, part],
        compiler_params=pltpu.CompilerParams(vmem_limit_bytes=4 * MIB),
        name="join_chip",
    )(me, own, mate, start)


def sides_kernel(me_ref, near_ref, far_ref, mask_ref, start_ref, side_ref, from_ref):
    narrow = start_ref[...].astype(jnp.bfloat16)
    chip_head, chip_tail = mask_ref[6:7], mask_ref[7:8]
    line = jnp.zeros_like(chip_head)
    left = right = (jnp.zeros(start_ref.shape, jnp.float32), line, line)
    from_ref[...] = jnp.zeros_like(from_ref)
    for i, (ref, up) in enumerate(zip((near_ref, far_ref), upward(me_ref[0]))):
        got = block_at(ref, 0)
        from_left = jnp.where(up, 0.0, flag(got[3] == chip_head))
        from_right = jnp.where(up, flag(got[3] == chip_tail), 0.0)
        from_ref[2 * i : 2 * i + 1] = from_left
        from_ref[2 * i + 1 : 2 * i + 2] = from_right
        left = join(narrow, left, got, from_left)
        right = join(narrow, right, got, from_right)
    put_block(side_ref, 0, left, line)
    put_block(side_ref, 2 * DIRS, right, line)


def join_sides(me, near, far, masks, start):
    width = near.shape[1]
    return pl.pallas_call(
        sides_kernel,
        in_specs=smem(1) + vmem(4),
        out_specs=vmem(2),
        out_shape=[
            jax.ShapeDtypeStruct((4 * DIRS, width), jnp.float32),
            jax.ShapeDtypeStruct((DIRS, width), jnp.float32),
        ],
        compiler_params=pltpu.CompilerParams(vmem_limit_bytes=4 * MIB),
        name="join_sides",
    )(me, near, far, masks, start)


def first_kernel(
    label_ref, image_ref, mean_ref, mate_ref, side_ref, other_ref, mask_ref, start_ref, spread_ref,
    out_ref, ends_ref, shift_ref,
):
    units = image_ref.shape[0]
    same, at_first, at_last = flags(label_ref)
    narrow = start_ref[...].astype(jnp.bfloat16)
    outer = []
    for first, mate_first, row in ((0, 2 * DIRS, 0), (2 * DIRS, 0, 1)):
        side = join(narrow, block_at(side_ref, first), block_at(other_ref, first), 1.0)
        mask = mask_ref[4 + row : 5 + row]
        side = side[0] * mask, side[1], side[2] * mask
        outer.append(join(narrow, side, block_at(mate_ref, mate_first), mask_ref[2 + row : 3 + row]))
    totals, shift = [], []
    for u in range(units):
        joined = join_units(u, same, narrow, image_ref, mean_ref)
        joined = join(narrow, joined, outer[0], at_first[u])
        joined = join(narrow, joined, outer[1], at_last[u])
        totals.append(joined[0])
        shift.append(mean_ref[u] - joined[1])
        shift_ref[u] = shift[u]
    multiply(totals, shift, same, spread_ref, out_ref, ends_ref)


def first_step(labels, images, means, mate, side, other, masks, start, spread):
    units, _, width = images.shape
    return pl.pallas_call(
        first_kernel,
        in_specs=smem(1) + vmem(8),
        out_specs=vmem(3),
        out_shape=image_shapes(units, width) + [jax.ShapeDtypeStruct((units, 1, width), jnp.float32)],
        compiler_params=pltpu.CompilerParams(vmem_limit_bytes=8 * MIB),
        name="first_step",
    )(labels, images, means, mate, side, other, masks, start, spread)


def step_kernel(label_ref, image_ref, first_ref, last_ref, shift_ref, spread_ref, out_ref, ends_ref):
    same, at_first, at_last = flags(label_ref)
    totals = whole_images(at_first, at_last, image_ref, first_ref, last_ref)
    shift = [shift_ref[u] for u in range(image_ref.shape[0])]
    multiply(totals, shift, same, spread_ref, out_ref, ends_ref)


def route_kernel(owner_ref, me_ref, label_ref, *refs):
    *refs, ends_ref, kept_ref = refs
    step_kernel(label_ref, *refs, ends_ref)
    images = [refs[-1][u] for u in range(refs[-1].shape[0])]
    core = me_ref[0] & 1
    count = kept_ref.shape[0] // DIRS
    for j in range(count):
        for ref, first, bit in ((kept_ref, 0, core), (ends_ref, 2 * DIRS, 1 - core)):
            owner = owner_ref[2 * j + bit]
            total = jnp.zeros_like(images[0])
            for u, image in enumerate(images):
                chosen = label_ref[u] == owner
                if u > 0:
                    chosen = chosen & (label_ref[u] != label_ref[u - 1])
                total = total + image * jnp.where(chosen, 1.0, 0.0)
            ref[first + j * DIRS : first + (j + 1) * DIRS] = total


def step(labels, images, first, last_image, shift, spread):
    units, _, width = images.shape
    return pl.pallas_call(
        step_kernel,
        in_specs=smem(1) + vmem(5),
        out_specs=vmem(2),
        out_shape=image_shapes(units, width),
        compiler_params=pltpu.CompilerParams(vmem_limit_bytes=8 * MIB),
        name="step",
    )(labels, images, first, last_image, shift, spread)


def step_and_route(owners, me, labels, images, first, last_image, shift, spread):
    units, _, width = images.shape
    tiles = owners.shape[0] // 2 * DIRS
    shapes = image_shapes(units, width)
    shapes[1] = jax.ShapeDtypeStruct((2 * DIRS + tiles, width), jnp.float32)
    shapes.append(jax.ShapeDtypeStruct((tiles, width), jnp.float32))
    return pl.pallas_call(
        route_kernel,
        in_specs=smem(3) + vmem(5),
        out_specs=vmem(3),
        out_shape=shapes,
        compiler_params=pltpu.CompilerParams(vmem_limit_bytes=8 * MIB),
        name="step_and_route",
    )(owners, me, labels, images, first, last_image, shift, spread)


def project_kernel(
    label_ref, image_ref, first_ref, last_ref, mean_ref, shift_ref, source, out_ref, x_ref, arrived
):
    copies = fetch(source, x_ref, arrived, 0, PART)
    _, at_first, at_last = flags(label_ref)
    totals = whole_images(at_first, at_last, image_ref, first_ref, last_ref)
    narrow = orthonormal(totals).astype(jnp.bfloat16)
    for i, copy in enumerate(copies):
        u = i * PART // UNIT
        chosen = narrow[u * DIRS : (u + 1) * DIRS]
        mean = mean_ref[u] - shift_ref[u]
        offset = jnp.sum(chosen.astype(jnp.float32) * mean, axis=1, keepdims=True)
        copy.wait()
        rows = slice(i * PART, (i + 1) * PART)
        out_ref[:, rows] = dot(chosen, x_ref[rows], ((1,), (1,))) - offset


def project(labels, images, first, last_image, means, shift, x):
    rows, width = x.shape
    return pl.pallas_call(
        project_kernel,
        in_specs=smem(1) + vmem(5) + [pl.BlockSpec(memory_space=pl.ANY)],
        out_specs=vmem(1)[0],
        out_shape=jax.ShapeDtypeStruct((DIRS, rows), jnp.float32),
        scratch_shapes=[pltpu.VMEM(x.shape, x.dtype), pltpu.SemaphoreType.DMA((rows // PART,))],
        compiler_params=pltpu.CompilerParams(vmem_limit_bytes=24 * MIB),
        cost_estimate=pl.CostEstimate(
            flops=2 * rows * width * 256, bytes_accessed=2 * rows * width, transcendentals=0
        ),
        name="project",
    )(labels, images, first, last_image, means, shift, x)


def finish_kernel(kept_ref, got_ref, out_ref):
    out_ref[0] = orthonormal([kept_ref[0] + got_ref[0]])


def finish(kept, got):
    return pl.pallas_call(
        finish_kernel,
        in_specs=vmem(2),
        out_specs=vmem(1)[0],
        out_shape=jax.ShapeDtypeStruct(kept.shape, jnp.float32),
        compiler_params=pltpu.CompilerParams(vmem_limit_bytes=4 * MIB),
        name="finish",
    )(kept, got)


def per_device(n_dp, embeddings, cluster_ids, owner_table, start_basis):
    rows, width = embeddings.shape
    units = rows // UNIT
    chips = n_dp // 2
    me = lax.axis_index("dp")
    labels = cluster_ids[::UNIT]

    near = (lambda p: p ^ 1, lambda p: (p + 1) % chips if p % 2 else (p - 1) % chips)
    far = (lambda p: p ^ 2, lambda p: (p + 2) % chips if p % 4 >= 2 else (p - 2) % chips)
    links = [
        [(2 * p + c, 2 * pairing[c](p) + c) for p in range(chips) for c in range(2)]
        for pairing in (near, far)
    ]
    mates = [(i, i ^ 1) for i in range(n_dp)]

    def halves(both):
        return both[:DIRS], both[DIRS:]

    def swap(both):
        return halves(lax.ppermute(both, "dp", mates))

    def chip_totals(own, mate, joins, even):
        head = jnp.where(even, own[0] + joins[0] * mate[0], mate[0] + joins[0] * own[0])
        tail = jnp.where(even, mate[1] + joins[1] * own[1], own[1] + joins[1] * mate[1])
        return head, tail

    def collect(left, right, own_side, mate, masks):
        mate_left, mate_right, at_head, at_tail = masks
        mate_side = swap(jnp.concatenate([left, right]))
        first = at_head * (left + mate_side[0]) + mate_left * mate[1]
        last_image = at_tail * (right + mate_side[1]) + mate_right * mate[0]
        return first, last_image

    embeddings = pltpu.with_memory_space_constraint(embeddings, pltpu.HBM)
    place = me.reshape(1)
    spread, raw, means, own = unit_spread(place, labels, embeddings, start_basis)

    mate = lax.ppermute(own, "dp", mates)
    near, far, masks = join_chip(place, own, mate, start_basis)
    near, far = (lax.ppermute(part, "dp", link) for part, link in zip((near, far), links))
    side, origins = join_sides(place, near, far, masks, start_basis)
    other = lax.ppermute(side, "dp", mates)
    images, ends, shift = first_step(
        labels, raw, means, mate, side, other, masks, start_basis, spread
    )
    joins = masks[0:1], masks[1:2]
    even, *ups = (masks[i : i + 1] > 0.5 for i in range(8, 11))
    masks = tuple(masks[i : i + 1] for i in range(2, 6))
    sides = [(origins[i : i + 1], origins[i + 1 : i + 2]) for i in (0, 2)]

    def exchange(ends, mate=None, beside=lambda: ()):
        mate, own = mate or swap(ends), halves(ends)
        totals = chip_totals(own, mate, joins, even)
        arrived = [
            lax.ppermute(jnp.where(up, totals[1], totals[0]), "dp", link) for link, up in zip(links, ups)
        ]
        arrived, other = lax.optimization_barrier((arrived, beside()))
        left = right = jnp.zeros_like(own[0])
        for got, (from_left, from_right) in zip(arrived, sides):
            left = left + from_left * got
            right = right + from_right * got
        return *collect(left, right, own, mate, masks), other

    def halve(tiles, bit):
        low, high = tiles[0::2], tiles[1::2]
        set_here = (me & bit) != 0
        return jnp.where(set_here, high, low), jnp.where(set_here, low, high)

    def route(sent, bit):
        return lax.ppermute(sent, "dp", [(i, i ^ bit) for i in range(n_dp)])

    def split(tiles, bit):
        kept, sent = halve(tiles, bit)
        return kept + route(sent, bit)

    for _ in range(ITERS - 3):
        images, ends = step(labels, images, *exchange(ends)[:2], shift, spread)

    images, ends, kept = step_and_route(
        owner_table, place, labels, images, *exchange(ends)[:2], shift, spread
    )
    got = lax.ppermute(ends, "dp", mates)
    kept = (kept + got[2 * DIRS :]).reshape(n_dp // 2, DIRS, width)
    kept, sent = halve(kept, 2)
    first, last_image, got = exchange(ends[: 2 * DIRS], halves(got[: 2 * DIRS]), lambda: route(sent, 2))
    kept = kept + got
    bit = 4
    while 2 * bit < n_dp:
        kept = split(kept, bit)
        bit *= 2
    kept, sent = halve(kept, bit)
    got = route(sent, bit)
    projections = project(labels, images, first, last_image, means, shift, embeddings)
    return finish(kept, got), projections


def solution(mesh):
    in_specs = (P(("groups", "dp"), None), P(("groups", "dp")), P("groups"), P())
    out_specs = (P(("groups", "dp"), None, None), P(None, ("groups", "dp")))
    body = functools.partial(per_device, mesh.shape["dp"])
    return jax.shard_map(body, mesh=mesh, in_specs=in_specs, out_specs=out_specs, check_vma=False)
```

```python
import functools

import jax
import jax.numpy as jnp
from jax import lax
from jax.experimental import pallas as pl
from jax.experimental.pallas import tpu as pltpu
from jax.sharding import PartitionSpec as P

DIRS = 8
ITERS = 6
UNIT = 2048
HIGHEST = lax.Precision.HIGHEST
BLOCK = 256
PART = 1024
MIB = 1024 * 1024


def dot(a, b, contract=((1,), (0,)), precision=None):
    return lax.dot_general(
        a, b, (contract, ((), ())), precision=precision, preferred_element_type=jnp.float32
    )


def apply_unit(narrow, spread_ref, u):
    return dot(narrow, spread_ref[0, u]) + dot(narrow, spread_ref[1, u])


def spread_kernel(
    _, label_ref, source, start_ref, spread_ref, image_ref, mean_ref, ends_ref, x_ref, centered, arrived
):
    u = pl.program_id(0)
    width = centered.shape[1]

    def copy(v):
        part = pl.ds(pl.multiple_of(v * UNIT, UNIT), UNIT)
        return pltpu.make_async_copy(source.at[part], x_ref.at[part], arrived.at[v])

    @pl.when(u == 0)
    def _():
        copy(0).start()

    def rows(a, size):
        return x_ref[pl.ds(pl.multiple_of(u * UNIT + a, BLOCK), size)]

    copy(u).wait()

    @pl.when(u + 1 < pl.num_programs(0))
    def _():
        copy(u + 1).start()

    ones = jnp.ones((DIRS, UNIT), jnp.bfloat16)
    mean = dot(ones, rows(0, UNIT))[:1] * (1 / UNIT)
    mean_ref[u] = mean
    for a in range(0, UNIT, BLOCK):
        centered[a : a + BLOCK] = (rows(a, BLOCK).astype(jnp.float32) - mean).astype(jnp.bfloat16)
    for a in range(0, width, BLOCK):
        spread = dot(centered[:, a : a + BLOCK], centered[:, a:], ((0,), (0,)))
        high = spread.astype(jnp.bfloat16)
        low = (spread - high.astype(jnp.float32)).astype(jnp.bfloat16)
        for h, part in enumerate((high, low)):
            spread_ref[h, u, a : a + BLOCK, a:] = part
            if a + BLOCK < width:
                spread_ref[h, u, a + BLOCK :, a : a + BLOCK] = part[:, BLOCK:].T
    narrow = start_ref[...].astype(jnp.bfloat16)
    image_ref[u] = apply_unit(narrow, spread_ref, u)

    @pl.when(u == pl.num_programs(0) - 1)
    def _():
        same, _, _ = flags(label_ref)
        units = image_ref.shape[0]
        for first, end in ((0, 0), (2 * DIRS, units - 1)):
            joined = join_units(end, same, narrow, image_ref, mean_ref)
            line = jnp.zeros_like(mean)
            parts = joined[0], joined[1], line + joined[2]
            put_block(ends_ref, first, parts, line + label_ref[end].astype(jnp.float32))


def join(narrow, a, b, mask):
    number = b[2] * mask
    total = a[2] + number
    share = number / jnp.maximum(total, 1.0)
    apart = b[1] - a[1]
    along = jnp.sum(narrow.astype(jnp.float32) * apart, axis=1, keepdims=True)
    images = a[0] + mask * b[0] + along * (UNIT * a[2] * share * apart)
    return images, a[1] + share * apart, total


def join_units(u, same, narrow, image_ref, mean_ref):
    joined = image_ref[u], mean_ref[u], jnp.float32(1.0)
    for v in range(image_ref.shape[0]):
        if v != u:
            joined = join(narrow, joined, (image_ref[v], mean_ref[v], jnp.float32(1.0)), same[u][v])
    return joined


def unit_spread(me, labels, x, start):
    rows, width = x.shape
    units = rows // UNIT
    return pl.pallas_call(
        spread_kernel,
        grid=(units,),
        in_specs=[
            *smem(2),
            pl.BlockSpec(memory_space=pl.ANY),
            pl.BlockSpec((DIRS, width), lambda u: (0, 0)),
        ],
        out_specs=vmem(5),
        out_shape=[
            pltpu.VMEM((2, units, width, width), jnp.bfloat16),
            jax.ShapeDtypeStruct((units, DIRS, width), jnp.float32),
            jax.ShapeDtypeStruct((units, 1, width), jnp.float32),
            jax.ShapeDtypeStruct((4 * DIRS, width), jnp.float32),
            pltpu.VMEM((rows, width), x.dtype),
        ],
        scratch_shapes=[pltpu.VMEM((UNIT, width), jnp.bfloat16), pltpu.SemaphoreType.DMA((units,))],
        compiler_params=pltpu.CompilerParams(vmem_limit_bytes=12 * MIB),
        name="unit_spread",
    )(me, labels, x, start)


def flags(label_ref):
    units = label_ref.shape[0]
    same = [
        [jnp.where(label_ref[u] == label_ref[v], 1.0, 0.0) for v in range(units)] for u in range(units)
    ]
    return same, [same[u][0] for u in range(units)], [same[u][units - 1] for u in range(units)]


def merge_units(images, narrow, shift, same, out_ref, ends_ref):
    units = len(images)
    full = []
    for u in range(units):
        along = jnp.sum(narrow[u].astype(jnp.float32) * shift[u], axis=1, keepdims=True)
        full.append(images[u] + (UNIT * along) * shift[u])
    for u in range(units):
        total = full[u]
        for v in range(units):
            if v != u:
                total = total + full[v] * same[u][v]
        out_ref[u] = total
        if u == 0:
            ends_ref[:DIRS] = total
        if u == units - 1:
            ends_ref[DIRS : 2 * DIRS] = total


def vmem(count):
    return [pl.BlockSpec(memory_space=pltpu.VMEM)] * count


def smem(count):
    return [pl.BlockSpec(memory_space=pltpu.SMEM)] * count


def image_shapes(units, width):
    return [
        jax.ShapeDtypeStruct((units, DIRS, width), jnp.float32),
        jax.ShapeDtypeStruct((2 * DIRS, width), jnp.float32),
    ]


def inverse_factor(images, row, lane):
    shape = row.shape
    columns = [
        jnp.broadcast_to(jnp.sum(images * images[j : j + 1], axis=1, keepdims=True), shape)
        for j in range(DIRS)
    ]
    inverse = (lane == row).astype(jnp.float32)
    scale = jnp.zeros(shape, jnp.float32)
    for k in range(DIRS):
        pivot = columns[k][k : k + 1]
        scale = jnp.where(row == k, lax.rsqrt(pivot), scale)
        factor = jnp.where(row > k, columns[k] * (1.0 / pivot), 0.0)
        inverse = inverse - factor * inverse[k : k + 1]
        for j in range(k + 1, DIRS):
            columns[j] = columns[j] - factor * columns[j][k : k + 1]
    return inverse * scale


def orthonormal(images):
    units = len(images)
    row = lax.broadcasted_iota(jnp.int32, (DIRS, units * DIRS), 0)
    lane = lax.broadcasted_iota(jnp.int32, (DIRS, units * DIRS), 1)
    inverse = [inverse_factor(images[u], row, lane - u * DIRS) for u in range(units)]
    return dot(jnp.concatenate(inverse, axis=0), jnp.concatenate(images, axis=0), precision=HIGHEST)


def whole_images(at_first, at_last, image_ref, first_ref, last_ref):
    first, last = first_ref[...], last_ref[...]
    return [
        image_ref[u] + first * at_first[u] + last * at_last[u] for u in range(image_ref.shape[0])
    ]


def multiply(totals, shift, same, spread_ref, out_ref, ends_ref):
    units = len(totals)
    basis = orthonormal(totals).astype(jnp.bfloat16)
    narrow = [basis[u * DIRS : (u + 1) * DIRS] for u in range(units)]
    images = [apply_unit(narrow[u], spread_ref, u) for u in range(units)]
    merge_units(images, narrow, shift, same, out_ref, ends_ref)


def block_at(ref, first):
    rest = first + DIRS
    return ref[first:rest], ref[rest : rest + 1], ref[rest + 1 : rest + 2], ref[rest + 2 : rest + 3]


def put_block(ref, first, parts, label):
    rest = first + DIRS
    ref[first:rest] = parts[0]
    for i, line in enumerate((parts[1], parts[2], label)):
        ref[rest + i : rest + i + 1] = line
    ref[rest + 3 : rest + DIRS] = jnp.zeros((DIRS - 3, ref.shape[1]), jnp.float32)


def upward(me):
    chip, core = me >> 1, me & 1
    return (chip & 1) == core, ((chip >> 1) & 1) == core


def flag(value):
    return jnp.where(value, 1.0, 0.0)


def chip_kernel(me_ref, own_ref, mate_ref, start_ref, near_ref, far_ref, mask_ref):
    even = (me_ref[0] & 1) == 0
    narrow = start_ref[...].astype(jnp.bfloat16)
    own = block_at(own_ref, 0), block_at(own_ref, 2 * DIRS)
    mate = block_at(mate_ref, 0), block_at(mate_ref, 2 * DIRS)
    head, tail, mate_head, mate_tail = own[0][3], own[1][3], mate[0][3], mate[1][3]
    chip_head = jnp.where(even, head, mate_head)
    chip_tail = jnp.where(even, mate_tail, tail)
    masks = [
        flag(head == mate_head),
        flag(tail == mate_tail),
        jnp.where(even, 0.0, flag(mate_tail == head)),
        jnp.where(even, flag(mate_head == tail), 0.0),
        flag(head == chip_head),
        flag(tail == chip_tail),
        chip_head,
        chip_tail,
        *(jnp.where(value, 1.0, jnp.zeros_like(head)) for value in (even, *upward(me_ref[0]))),
        *(jnp.where(((me_ref[0] >> b) & 1) == 1, 1.0, jnp.zeros_like(head)) for b in range(1, 6)),
    ]
    mask_ref[...] = jnp.zeros_like(mask_ref)
    for i, line in enumerate(masks):
        mask_ref[i : i + 1] = line

    def order(a, b):
        return [jnp.where(even, x, y) for x, y in zip(a, b)], [jnp.where(even, y, x) for x, y in zip(a, b)]

    at_head = join(narrow, *order(own[0], mate[0]), masks[0])
    at_tail = join(narrow, *order(mate[1], own[1]), masks[1])
    for ref, up in zip((near_ref, far_ref), upward(me_ref[0])):
        parts = [jnp.where(up, x, y) for x, y in zip(at_tail, at_head)]
        put_block(ref, 0, parts, jnp.where(up, chip_tail, chip_head))


def join_chip(me, own, mate, start):
    width = own.shape[1]
    part = jax.ShapeDtypeStruct((2 * DIRS, width), jnp.float32)
    return pl.pallas_call(
        chip_kernel,
        in_specs=smem(1) + vmem(3),
        out_specs=vmem(3),
        out_shape=[part, part, part],
        compiler_params=pltpu.CompilerParams(vmem_limit_bytes=4 * MIB),
        name="join_chip",
    )(me, own, mate, start)


def sides_kernel(me_ref, near_ref, far_ref, mask_ref, start_ref, side_ref, from_ref):
    narrow = start_ref[...].astype(jnp.bfloat16)
    chip_head, chip_tail = mask_ref[6:7], mask_ref[7:8]
    line = jnp.zeros_like(chip_head)
    left = right = (jnp.zeros(start_ref.shape, jnp.float32), line, line)
    from_ref[...] = jnp.zeros_like(from_ref)
    for i, (ref, up) in enumerate(zip((near_ref, far_ref), upward(me_ref[0]))):
        got = block_at(ref, 0)
        from_left = jnp.where(up, 0.0, flag(got[3] == chip_head))
        from_right = jnp.where(up, flag(got[3] == chip_tail), 0.0)
        from_ref[2 * i : 2 * i + 1] = from_left
        from_ref[2 * i + 1 : 2 * i + 2] = from_right
        left = join(narrow, left, got, from_left)
        right = join(narrow, right, got, from_right)
    put_block(side_ref, 0, left, line)
    put_block(side_ref, 2 * DIRS, right, line)


def join_sides(me, near, far, masks, start):
    width = near.shape[1]
    return pl.pallas_call(
        sides_kernel,
        in_specs=smem(1) + vmem(4),
        out_specs=vmem(2),
        out_shape=[
            jax.ShapeDtypeStruct((4 * DIRS, width), jnp.float32),
            jax.ShapeDtypeStruct((DIRS, width), jnp.float32),
        ],
        compiler_params=pltpu.CompilerParams(vmem_limit_bytes=4 * MIB),
        name="join_sides",
    )(me, near, far, masks, start)


def first_kernel(
    label_ref, image_ref, mean_ref, mate_ref, side_ref, other_ref, mask_ref, start_ref, spread_ref,
    out_ref, ends_ref, shift_ref,
):
    units = image_ref.shape[0]
    same, at_first, at_last = flags(label_ref)
    narrow = start_ref[...].astype(jnp.bfloat16)
    outer = []
    for first, mate_first, row in ((0, 2 * DIRS, 0), (2 * DIRS, 0, 1)):
        side = join(narrow, block_at(side_ref, first), block_at(other_ref, first), 1.0)
        mask = mask_ref[4 + row : 5 + row]
        side = side[0] * mask, side[1], side[2] * mask
        outer.append(join(narrow, side, block_at(mate_ref, mate_first), mask_ref[2 + row : 3 + row]))
    totals, shift = [], []
    for u in range(units):
        joined = join_units(u, same, narrow, image_ref, mean_ref)
        joined = join(narrow, joined, outer[0], at_first[u])
        joined = join(narrow, joined, outer[1], at_last[u])
        totals.append(joined[0])
        shift.append(mean_ref[u] - joined[1])
        shift_ref[u] = shift[u]
    multiply(totals, shift, same, spread_ref, out_ref, ends_ref)


def first_step(labels, images, means, mate, side, other, masks, start, spread):
    units, _, width = images.shape
    return pl.pallas_call(
        first_kernel,
        in_specs=smem(1) + vmem(8),
        out_specs=vmem(3),
        out_shape=image_shapes(units, width) + [jax.ShapeDtypeStruct((units, 1, width), jnp.float32)],
        compiler_params=pltpu.CompilerParams(vmem_limit_bytes=8 * MIB),
        name="first_step",
    )(labels, images, means, mate, side, other, masks, start, spread)


def step_kernel(label_ref, image_ref, first_ref, last_ref, shift_ref, spread_ref, out_ref, ends_ref):
    same, at_first, at_last = flags(label_ref)
    totals = whole_images(at_first, at_last, image_ref, first_ref, last_ref)
    shift = [shift_ref[u] for u in range(image_ref.shape[0])]
    multiply(totals, shift, same, spread_ref, out_ref, ends_ref)


def route_kernel(owner_ref, me_ref, label_ref, *refs):
    *refs, ends_ref, kept_ref = refs
    step_kernel(label_ref, *refs, ends_ref)
    images = [refs[-1][u] for u in range(refs[-1].shape[0])]
    core = me_ref[0] & 1
    count = kept_ref.shape[0] // DIRS
    for j in range(count):
        for ref, first, bit in ((kept_ref, 0, core), (ends_ref, 2 * DIRS, 1 - core)):
            owner = owner_ref[2 * j + bit]
            total = jnp.zeros_like(images[0])
            for u, image in enumerate(images):
                chosen = label_ref[u] == owner
                if u > 0:
                    chosen = chosen & (label_ref[u] != label_ref[u - 1])
                total = total + image * jnp.where(chosen, 1.0, 0.0)
            ref[first + j * DIRS : first + (j + 1) * DIRS] = total


def step(labels, images, first, last_image, shift, spread):
    units, _, width = images.shape
    return pl.pallas_call(
        step_kernel,
        in_specs=smem(1) + vmem(5),
        out_specs=vmem(2),
        out_shape=image_shapes(units, width),
        compiler_params=pltpu.CompilerParams(vmem_limit_bytes=8 * MIB),
        name="step",
    )(labels, images, first, last_image, shift, spread)


def step_and_route(owners, me, labels, images, first, last_image, shift, spread):
    units, _, width = images.shape
    tiles = owners.shape[0] // 2 * DIRS
    shapes = image_shapes(units, width)
    shapes[1] = jax.ShapeDtypeStruct((2 * DIRS + tiles, width), jnp.float32)
    shapes.append(jax.ShapeDtypeStruct((tiles, width), jnp.float32))
    return pl.pallas_call(
        route_kernel,
        in_specs=smem(3) + vmem(5),
        out_specs=vmem(3),
        out_shape=shapes,
        compiler_params=pltpu.CompilerParams(vmem_limit_bytes=8 * MIB),
        name="step_and_route",
    )(owners, me, labels, images, first, last_image, shift, spread)


def project_kernel(label_ref, image_ref, first_ref, last_ref, mean_ref, shift_ref, x_ref, out_ref):
    _, at_first, at_last = flags(label_ref)
    totals = whole_images(at_first, at_last, image_ref, first_ref, last_ref)
    narrow = orthonormal(totals).astype(jnp.bfloat16)
    for start in range(0, x_ref.shape[0], PART):
        u = start // UNIT
        chosen = narrow[u * DIRS : (u + 1) * DIRS]
        mean = mean_ref[u] - shift_ref[u]
        offset = jnp.sum(chosen.astype(jnp.float32) * mean, axis=1, keepdims=True)
        rows = slice(start, start + PART)
        out_ref[:, rows] = dot(chosen, x_ref[rows], ((1,), (1,))) - offset


def project(labels, images, first, last_image, means, shift, x):
    rows, width = x.shape
    return pl.pallas_call(
        project_kernel,
        in_specs=smem(1) + vmem(6),
        out_specs=vmem(1)[0],
        out_shape=jax.ShapeDtypeStruct((DIRS, rows), jnp.float32),
        compiler_params=pltpu.CompilerParams(vmem_limit_bytes=8 * MIB),
        cost_estimate=pl.CostEstimate(
            flops=2 * rows * width * 256, bytes_accessed=2 * rows * width, transcendentals=0
        ),
        name="project",
    )(labels, images, first, last_image, means, shift, x)


def finish_kernel(kept_ref, got_ref, out_ref):
    out_ref[0] = orthonormal([kept_ref[0] + got_ref[0]])


def finish(kept, got):
    return pl.pallas_call(
        finish_kernel,
        in_specs=vmem(2),
        out_specs=vmem(1)[0],
        out_shape=jax.ShapeDtypeStruct(kept.shape, jnp.float32),
        compiler_params=pltpu.CompilerParams(vmem_limit_bytes=4 * MIB),
        name="finish",
    )(kept, got)


def per_device(n_dp, embeddings, cluster_ids, owner_table, start_basis):
    rows, width = embeddings.shape
    units = rows // UNIT
    chips = n_dp // 2
    me = lax.axis_index("dp")
    labels = cluster_ids[::UNIT]

    near = (lambda p: p ^ 1, lambda p: (p + 1) % chips if p % 2 else (p - 1) % chips)
    far = (lambda p: p ^ 2, lambda p: (p + 2) % chips if p % 4 >= 2 else (p - 2) % chips)
    links = [
        [(2 * p + c, 2 * pairing[c](p) + c) for p in range(chips) for c in range(2)]
        for pairing in (near, far)
    ]
    mates = [(i, i ^ 1) for i in range(n_dp)]

    def halves(both):
        return both[:DIRS], both[DIRS:]

    def swap(both):
        return halves(lax.ppermute(both, "dp", mates))

    def chip_totals(own, mate, joins, even):
        head = jnp.where(even, own[0] + joins[0] * mate[0], mate[0] + joins[0] * own[0])
        tail = jnp.where(even, mate[1] + joins[1] * own[1], own[1] + joins[1] * mate[1])
        return head, tail

    def collect(left, right, own_side, mate, masks):
        mate_left, mate_right, at_head, at_tail = masks
        mate_side = swap(jnp.concatenate([left, right]))
        first = at_head * (left + mate_side[0]) + mate_left * mate[1]
        last_image = at_tail * (right + mate_side[1]) + mate_right * mate[0]
        return first, last_image

    embeddings = pltpu.with_memory_space_constraint(embeddings, pltpu.HBM)
    place = me.reshape(1)
    spread, raw, means, own, rows_here = unit_spread(place, labels, embeddings, start_basis)

    mate = lax.ppermute(own, "dp", mates)
    near, far, masks = join_chip(place, own, mate, start_basis)
    near, far = (lax.ppermute(part, "dp", link) for part, link in zip((near, far), links))
    side, origins = join_sides(place, near, far, masks, start_basis)
    other = lax.ppermute(side, "dp", mates)
    images, ends, shift = first_step(
        labels, raw, means, mate, side, other, masks, start_basis, spread
    )
    joins = masks[0:1], masks[1:2]
    even, *ups = (masks[i : i + 1] > 0.5 for i in range(8, 11))
    bits = {1 << b: masks[10 + b : 11 + b] > 0.5 for b in range(1, 6)}
    masks = tuple(masks[i : i + 1] for i in range(2, 6))
    sides = [(origins[i : i + 1], origins[i + 1 : i + 2]) for i in (0, 2)]

    def exchange(ends, mate=None, beside=lambda: ()):
        mate, own = mate or swap(ends), halves(ends)
        totals = chip_totals(own, mate, joins, even)
        arrived = [
            lax.ppermute(jnp.where(up, totals[1], totals[0]), "dp", link) for link, up in zip(links, ups)
        ]
        arrived, other = lax.optimization_barrier((arrived, beside()))
        left = right = jnp.zeros_like(own[0])
        for got, (from_left, from_right) in zip(arrived, sides):
            left = left + from_left * got
            right = right + from_right * got
        return *collect(left, right, own, mate, masks), other

    def halve(tiles, bit):
        low, high = tiles[0::2], tiles[1::2]
        set_here = bits[bit]
        return jnp.where(set_here, high, low), jnp.where(set_here, low, high)

    def route(sent, bit):
        return lax.ppermute(sent, "dp", [(i, i ^ bit) for i in range(n_dp)])

    def split(tiles, bit):
        kept, sent = halve(tiles, bit)
        return kept + route(sent, bit)

    for _ in range(ITERS - 3):
        images, ends = step(labels, images, *exchange(ends)[:2], shift, spread)

    images, ends, kept = step_and_route(
        owner_table, place, labels, images, *exchange(ends)[:2], shift, spread
    )
    got = lax.ppermute(ends, "dp", mates)
    kept = (kept + got[2 * DIRS :]).reshape(n_dp // 2, DIRS, width)
    kept, sent = halve(kept, 2)
    first, last_image, got = exchange(ends[: 2 * DIRS], halves(got[: 2 * DIRS]), lambda: route(sent, 2))
    kept = kept + got
    bit = 4
    while 2 * bit < n_dp:
        kept = split(kept, bit)
        bit *= 2
    kept, sent = halve(kept, bit)
    got = route(sent, bit)
    projections = project(labels, images, first, last_image, means, shift, rows_here)
    return finish(kept, got), projections


def solution(mesh):
    in_specs = (P(("groups", "dp"), None), P(("groups", "dp")), P("groups"), P())
    out_specs = (P(("groups", "dp"), None, None), P(None, ("groups", "dp")))
    body = functools.partial(per_device, mesh.shape["dp"])
    return jax.shard_map(body, mesh=mesh, in_specs=in_specs, out_specs=out_specs, check_vma=False)
```

```python
import functools

import jax
import jax.numpy as jnp
from jax import lax
from jax.experimental import pallas as pl
from jax.experimental.pallas import tpu as pltpu
from jax.sharding import PartitionSpec as P

DIRS = 8
ITERS = 6
UNIT = 2048
HIGHEST = lax.Precision.HIGHEST
BLOCK = 256
PART = 1024
MIB = 1024 * 1024


def dot(a, b, contract=((1,), (0,)), precision=None):
    return lax.dot_general(
        a, b, (contract, ((), ())), precision=precision, preferred_element_type=jnp.float32
    )


def apply_unit(narrow, spread_ref, u):
    return dot(narrow, spread_ref[0, u]) + dot(narrow, spread_ref[1, u])


def spread_kernel(
    _, label_ref, source, start_ref, spread_ref, image_ref, mean_ref, ends_ref, x_ref, centered, arrived
):
    u = pl.program_id(0)
    width = centered.shape[1]

    def copy(v):
        part = pl.ds(pl.multiple_of(v * UNIT, UNIT), UNIT)
        return pltpu.make_async_copy(source.at[part], x_ref.at[part], arrived.at[v])

    @pl.when(u == 0)
    def _():
        copy(0).start()

    def rows(a, size):
        return x_ref[pl.ds(pl.multiple_of(u * UNIT + a, BLOCK), size)]

    copy(u).wait()

    @pl.when(u + 1 < pl.num_programs(0))
    def _():
        copy(u + 1).start()

    ones = jnp.ones((DIRS, UNIT), jnp.bfloat16)
    mean = dot(ones, rows(0, UNIT))[:1] * (1 / UNIT)
    mean_ref[u] = mean
    for a in range(0, UNIT, BLOCK):
        centered[a : a + BLOCK] = (rows(a, BLOCK).astype(jnp.float32) - mean).astype(jnp.bfloat16)
    for a in range(0, width, BLOCK):
        spread = dot(centered[:, a : a + BLOCK], centered[:, a:], ((0,), (0,)))
        high = spread.astype(jnp.bfloat16)
        low = (spread - high.astype(jnp.float32)).astype(jnp.bfloat16)
        for h, part in enumerate((high, low)):
            spread_ref[h, u, a : a + BLOCK, a:] = part
            if a + BLOCK < width:
                spread_ref[h, u, a + BLOCK :, a : a + BLOCK] = part[:, BLOCK:].T
    narrow = start_ref[...].astype(jnp.bfloat16)
    image_ref[u] = apply_unit(narrow, spread_ref, u)

    @pl.when(u == pl.num_programs(0) - 1)
    def _():
        same, _, _ = flags(label_ref)
        units = image_ref.shape[0]
        for first, end in ((0, 0), (2 * DIRS, units - 1)):
            joined = join_units(end, same, narrow, image_ref, mean_ref)
            line = jnp.zeros_like(mean)
            parts = joined[0], joined[1], line + joined[2]
            put_block(ends_ref, first, parts, line + label_ref[end].astype(jnp.float32))


def join(narrow, a, b, mask):
    number = b[2] * mask
    total = a[2] + number
    share = number / jnp.maximum(total, 1.0)
    apart = b[1] - a[1]
    along = jnp.sum(narrow.astype(jnp.float32) * apart, axis=1, keepdims=True)
    images = a[0] + mask * b[0] + along * (UNIT * a[2] * share * apart)
    return images, a[1] + share * apart, total


def join_units(u, same, narrow, image_ref, mean_ref):
    joined = image_ref[u], mean_ref[u], jnp.float32(1.0)
    for v in range(image_ref.shape[0]):
        if v != u:
            joined = join(narrow, joined, (image_ref[v], mean_ref[v], jnp.float32(1.0)), same[u][v])
    return joined


def unit_spread(me, labels, x, start):
    rows, width = x.shape
    units = rows // UNIT
    return pl.pallas_call(
        spread_kernel,
        grid=(units,),
        in_specs=[
            *smem(2),
            pl.BlockSpec(memory_space=pl.ANY),
            pl.BlockSpec((DIRS, width), lambda u: (0, 0)),
        ],
        out_specs=vmem(5),
        out_shape=[
            pltpu.VMEM((2, units, width, width), jnp.bfloat16),
            jax.ShapeDtypeStruct((units, DIRS, width), jnp.float32),
            jax.ShapeDtypeStruct((units, 1, width), jnp.float32),
            jax.ShapeDtypeStruct((4 * DIRS, width), jnp.float32),
            pltpu.VMEM((rows, width), x.dtype),
        ],
        scratch_shapes=[pltpu.VMEM((UNIT, width), jnp.bfloat16), pltpu.SemaphoreType.DMA((units,))],
        compiler_params=pltpu.CompilerParams(vmem_limit_bytes=12 * MIB),
        name="unit_spread",
    )(me, labels, x, start)


def flags(label_ref):
    units = label_ref.shape[0]
    same = [
        [jnp.where(label_ref[u] == label_ref[v], 1.0, 0.0) for v in range(units)] for u in range(units)
    ]
    return same, [same[u][0] for u in range(units)], [same[u][units - 1] for u in range(units)]


def merge_units(images, narrow, shift, same, out_ref, ends_ref):
    units = len(images)
    full = []
    for u in range(units):
        along = jnp.sum(narrow[u].astype(jnp.float32) * shift[u], axis=1, keepdims=True)
        full.append(images[u] + (UNIT * along) * shift[u])
    for u in range(units):
        total = full[u]
        for v in range(units):
            if v != u:
                total = total + full[v] * same[u][v]
        out_ref[u] = total
        if u == 0:
            ends_ref[:DIRS] = total
        if u == units - 1:
            ends_ref[DIRS : 2 * DIRS] = total


def vmem(count):
    return [pl.BlockSpec(memory_space=pltpu.VMEM)] * count


def smem(count):
    return [pl.BlockSpec(memory_space=pltpu.SMEM)] * count


def image_shapes(units, width):
    return [
        jax.ShapeDtypeStruct((units, DIRS, width), jnp.float32),
        jax.ShapeDtypeStruct((2 * DIRS, width), jnp.float32),
    ]


def inverse_factor(images, row, lane):
    shape = row.shape
    columns = [
        jnp.broadcast_to(jnp.sum(images * images[j : j + 1], axis=1, keepdims=True), shape)
        for j in range(DIRS)
    ]
    inverse = (lane == row).astype(jnp.float32)
    scale = jnp.zeros(shape, jnp.float32)
    for k in range(DIRS):
        pivot = columns[k][k : k + 1]
        scale = jnp.where(row == k, lax.rsqrt(pivot), scale)
        factor = jnp.where(row > k, columns[k] * (1.0 / pivot), 0.0)
        inverse = inverse - factor * inverse[k : k + 1]
        for j in range(k + 1, DIRS):
            columns[j] = columns[j] - factor * columns[j][k : k + 1]
    return inverse * scale


def orthonormal(images):
    units = len(images)
    row = lax.broadcasted_iota(jnp.int32, (DIRS, units * DIRS), 0)
    lane = lax.broadcasted_iota(jnp.int32, (DIRS, units * DIRS), 1)
    inverse = [inverse_factor(images[u], row, lane - u * DIRS) for u in range(units)]
    return dot(jnp.concatenate(inverse, axis=0), jnp.concatenate(images, axis=0), precision=HIGHEST)


def whole_images(at_first, at_last, image_ref, first_ref, last_ref):
    first, last = first_ref[...], last_ref[...]
    return [
        image_ref[u] + first * at_first[u] + last * at_last[u] for u in range(image_ref.shape[0])
    ]


def multiply(totals, shift, same, spread_ref, out_ref, ends_ref):
    units = len(totals)
    basis = orthonormal(totals).astype(jnp.bfloat16)
    narrow = [basis[u * DIRS : (u + 1) * DIRS] for u in range(units)]
    images = [apply_unit(narrow[u], spread_ref, u) for u in range(units)]
    merge_units(images, narrow, shift, same, out_ref, ends_ref)


def block_at(ref, first):
    rest = first + DIRS
    return ref[first:rest], ref[rest : rest + 1], ref[rest + 1 : rest + 2], ref[rest + 2 : rest + 3]


def put_block(ref, first, parts, label):
    rest = first + DIRS
    ref[first:rest] = parts[0]
    for i, line in enumerate((parts[1], parts[2], label)):
        ref[rest + i : rest + i + 1] = line
    ref[rest + 3 : rest + DIRS] = jnp.zeros((DIRS - 3, ref.shape[1]), jnp.float32)


def upward(me):
    chip, core = me >> 1, me & 1
    return (chip & 1) == core, ((chip >> 1) & 1) == core


def flag(value):
    return jnp.where(value, 1.0, 0.0)


def chip_kernel(me_ref, own_ref, mate_ref, start_ref, near_ref, far_ref, mask_ref):
    even = (me_ref[0] & 1) == 0
    narrow = start_ref[...].astype(jnp.bfloat16)
    own = block_at(own_ref, 0), block_at(own_ref, 2 * DIRS)
    mate = block_at(mate_ref, 0), block_at(mate_ref, 2 * DIRS)
    head, tail, mate_head, mate_tail = own[0][3], own[1][3], mate[0][3], mate[1][3]
    chip_head = jnp.where(even, head, mate_head)
    chip_tail = jnp.where(even, mate_tail, tail)
    masks = [
        flag(head == mate_head),
        flag(tail == mate_tail),
        jnp.where(even, 0.0, flag(mate_tail == head)),
        jnp.where(even, flag(mate_head == tail), 0.0),
        flag(head == chip_head),
        flag(tail == chip_tail),
        chip_head,
        chip_tail,
        *(jnp.where(value, 1.0, jnp.zeros_like(head)) for value in (even, *upward(me_ref[0]))),
        *(jnp.where(((me_ref[0] >> b) & 1) == 1, 1.0, jnp.zeros_like(head)) for b in range(1, 6)),
    ]
    mask_ref[...] = jnp.zeros_like(mask_ref)
    for i, line in enumerate(masks):
        mask_ref[i : i + 1] = line

    def order(a, b):
        return [jnp.where(even, x, y) for x, y in zip(a, b)], [jnp.where(even, y, x) for x, y in zip(a, b)]

    at_head = join(narrow, *order(own[0], mate[0]), masks[0])
    at_tail = join(narrow, *order(mate[1], own[1]), masks[1])
    for ref, up in zip((near_ref, far_ref), upward(me_ref[0])):
        parts = [jnp.where(up, x, y) for x, y in zip(at_tail, at_head)]
        put_block(ref, 0, parts, jnp.where(up, chip_tail, chip_head))


def join_chip(me, own, mate, start):
    width = own.shape[1]
    part = jax.ShapeDtypeStruct((2 * DIRS, width), jnp.float32)
    return pl.pallas_call(
        chip_kernel,
        in_specs=smem(1) + vmem(3),
        out_specs=vmem(3),
        out_shape=[part, part, part],
        compiler_params=pltpu.CompilerParams(vmem_limit_bytes=4 * MIB),
        name="join_chip",
    )(me, own, mate, start)


def sides_kernel(me_ref, near_ref, far_ref, mask_ref, start_ref, side_ref, from_ref):
    narrow = start_ref[...].astype(jnp.bfloat16)
    chip_head, chip_tail = mask_ref[6:7], mask_ref[7:8]
    line = jnp.zeros_like(chip_head)
    left = right = (jnp.zeros(start_ref.shape, jnp.float32), line, line)
    from_ref[...] = jnp.zeros_like(from_ref)
    for i, (ref, up) in enumerate(zip((near_ref, far_ref), upward(me_ref[0]))):
        got = block_at(ref, 0)
        from_left = jnp.where(up, 0.0, flag(got[3] == chip_head))
        from_right = jnp.where(up, flag(got[3] == chip_tail), 0.0)
        from_ref[2 * i : 2 * i + 1] = from_left
        from_ref[2 * i + 1 : 2 * i + 2] = from_right
        left = join(narrow, left, got, from_left)
        right = join(narrow, right, got, from_right)
    put_block(side_ref, 0, left, line)
    put_block(side_ref, 2 * DIRS, right, line)


def join_sides(me, near, far, masks, start):
    width = near.shape[1]
    return pl.pallas_call(
        sides_kernel,
        in_specs=smem(1) + vmem(4),
        out_specs=vmem(2),
        out_shape=[
            jax.ShapeDtypeStruct((4 * DIRS, width), jnp.float32),
            jax.ShapeDtypeStruct((DIRS, width), jnp.float32),
        ],
        compiler_params=pltpu.CompilerParams(vmem_limit_bytes=4 * MIB),
        name="join_sides",
    )(me, near, far, masks, start)


def first_kernel(
    label_ref, image_ref, mean_ref, mate_ref, side_ref, other_ref, mask_ref, start_ref, spread_ref,
    out_ref, ends_ref, shift_ref,
):
    units = image_ref.shape[0]
    same, at_first, at_last = flags(label_ref)
    narrow = start_ref[...].astype(jnp.bfloat16)
    outer = []
    for first, mate_first, row in ((0, 2 * DIRS, 0), (2 * DIRS, 0, 1)):
        side = join(narrow, block_at(side_ref, first), block_at(other_ref, first), 1.0)
        mask = mask_ref[4 + row : 5 + row]
        side = side[0] * mask, side[1], side[2] * mask
        outer.append(join(narrow, side, block_at(mate_ref, mate_first), mask_ref[2 + row : 3 + row]))
    totals, shift = [], []
    for u in range(units):
        joined = join_units(u, same, narrow, image_ref, mean_ref)
        joined = join(narrow, joined, outer[0], at_first[u])
        joined = join(narrow, joined, outer[1], at_last[u])
        totals.append(joined[0])
        shift.append(mean_ref[u] - joined[1])
        shift_ref[u] = shift[u]
    multiply(totals, shift, same, spread_ref, out_ref, ends_ref)


def first_step(labels, images, means, mate, side, other, masks, start, spread):
    units, _, width = images.shape
    return pl.pallas_call(
        first_kernel,
        in_specs=smem(1) + vmem(8),
        out_specs=vmem(3),
        out_shape=image_shapes(units, width) + [jax.ShapeDtypeStruct((units, 1, width), jnp.float32)],
        compiler_params=pltpu.CompilerParams(vmem_limit_bytes=8 * MIB),
        name="first_step",
    )(labels, images, means, mate, side, other, masks, start, spread)


def step_kernel(label_ref, image_ref, first_ref, last_ref, shift_ref, spread_ref, out_ref, ends_ref):
    same, at_first, at_last = flags(label_ref)
    totals = whole_images(at_first, at_last, image_ref, first_ref, last_ref)
    shift = [shift_ref[u] for u in range(image_ref.shape[0])]
    multiply(totals, shift, same, spread_ref, out_ref, ends_ref)


def route_kernel(owner_ref, me_ref, label_ref, *refs):
    *refs, ends_ref, kept_ref = refs
    step_kernel(label_ref, *refs, ends_ref)
    images = [refs[-1][u] for u in range(refs[-1].shape[0])]
    core = me_ref[0] & 1
    count = kept_ref.shape[0] // DIRS
    for j in range(count):
        for ref, first, bit in ((kept_ref, 0, core), (ends_ref, 2 * DIRS, 1 - core)):
            owner = owner_ref[2 * j + bit]
            total = jnp.zeros_like(images[0])
            for u, image in enumerate(images):
                chosen = label_ref[u] == owner
                if u > 0:
                    chosen = chosen & (label_ref[u] != label_ref[u - 1])
                total = total + image * jnp.where(chosen, 1.0, 0.0)
            ref[first + j * DIRS : first + (j + 1) * DIRS] = total


def step(labels, images, first, last_image, shift, spread):
    units, _, width = images.shape
    return pl.pallas_call(
        step_kernel,
        in_specs=smem(1) + vmem(5),
        out_specs=vmem(2),
        out_shape=image_shapes(units, width),
        compiler_params=pltpu.CompilerParams(vmem_limit_bytes=8 * MIB),
        name="step",
    )(labels, images, first, last_image, shift, spread)


def step_and_route(owners, me, labels, images, first, last_image, shift, spread):
    units, _, width = images.shape
    tiles = owners.shape[0] // 2 * DIRS
    shapes = image_shapes(units, width)
    shapes[1] = jax.ShapeDtypeStruct((2 * DIRS + tiles, width), jnp.float32)
    shapes.append(jax.ShapeDtypeStruct((tiles, width), jnp.float32))
    return pl.pallas_call(
        route_kernel,
        in_specs=smem(3) + vmem(5),
        out_specs=vmem(3),
        out_shape=shapes,
        compiler_params=pltpu.CompilerParams(vmem_limit_bytes=8 * MIB),
        name="step_and_route",
    )(owners, me, labels, images, first, last_image, shift, spread)


def project_kernel(label_ref, image_ref, first_ref, last_ref, mean_ref, shift_ref, x_ref, out_ref):
    _, at_first, at_last = flags(label_ref)
    totals = whole_images(at_first, at_last, image_ref, first_ref, last_ref)
    narrow = orthonormal(totals).astype(jnp.bfloat16)
    for start in range(0, x_ref.shape[0], PART):
        u = start // UNIT
        chosen = narrow[u * DIRS : (u + 1) * DIRS]
        mean = mean_ref[u] - shift_ref[u]
        offset = jnp.sum(chosen.astype(jnp.float32) * mean, axis=1, keepdims=True)
        rows = slice(start, start + PART)
        out_ref[:, rows] = dot(chosen, x_ref[rows], ((1,), (1,))) - offset


def project(labels, images, first, last_image, means, shift, x):
    rows, width = x.shape
    return pl.pallas_call(
        project_kernel,
        in_specs=smem(1) + vmem(6),
        out_specs=vmem(1)[0],
        out_shape=jax.ShapeDtypeStruct((DIRS, rows), jnp.float32),
        compiler_params=pltpu.CompilerParams(vmem_limit_bytes=8 * MIB),
        cost_estimate=pl.CostEstimate(
            flops=2 * rows * width * 256, bytes_accessed=2 * rows * width, transcendentals=0
        ),
        name="project",
    )(labels, images, first, last_image, means, shift, x)


def finish_kernel(kept_ref, got_ref, out_ref):
    out_ref[0] = orthonormal([kept_ref[0] + got_ref[0]])


def finish(kept, got):
    return pl.pallas_call(
        finish_kernel,
        in_specs=vmem(2),
        out_specs=vmem(1)[0],
        out_shape=jax.ShapeDtypeStruct(kept.shape, jnp.float32),
        compiler_params=pltpu.CompilerParams(vmem_limit_bytes=4 * MIB),
        name="finish",
    )(kept, got)


def per_device(n_dp, embeddings, cluster_ids, owner_table, start_basis):
    rows, width = embeddings.shape
    units = rows // UNIT
    chips = n_dp // 2
    me = lax.axis_index("dp")
    labels = cluster_ids[::UNIT]

    near = (lambda p: p ^ 1, lambda p: (p + 1) % chips if p % 2 else (p - 1) % chips)
    far = (lambda p: p ^ 2, lambda p: (p + 2) % chips if p % 4 >= 2 else (p - 2) % chips)
    links = [
        [(2 * p + c, 2 * pairing[c](p) + c) for p in range(chips) for c in range(2)]
        for pairing in (near, far)
    ]
    mates = [(i, i ^ 1) for i in range(n_dp)]

    def halves(both):
        return both[:DIRS], both[DIRS:]

    def swap(both):
        return halves(lax.ppermute(both, "dp", mates))

    def chip_totals(own, mate, joins, even):
        head = jnp.where(even, own[0] + joins[0] * mate[0], mate[0] + joins[0] * own[0])
        tail = jnp.where(even, mate[1] + joins[1] * own[1], own[1] + joins[1] * mate[1])
        return head, tail

    def collect(left, right, own_side, mate, masks):
        mate_left, mate_right, at_head, at_tail = masks
        mate_side = swap(jnp.concatenate([left, right]))
        first = at_head * (left + mate_side[0]) + mate_left * mate[1]
        last_image = at_tail * (right + mate_side[1]) + mate_right * mate[0]
        return first, last_image

    embeddings = pltpu.with_memory_space_constraint(embeddings, pltpu.HBM)
    place = me.reshape(1)
    spread, raw, means, own, rows_here = unit_spread(
        place, labels, embeddings, pltpu.with_memory_space_constraint(start_basis, pltpu.HBM)
    )

    mate = lax.ppermute(own, "dp", mates)
    near, far, masks = join_chip(place, own, mate, start_basis)
    near, far = (lax.ppermute(part, "dp", link) for part, link in zip((near, far), links))
    side, origins = join_sides(place, near, far, masks, start_basis)
    other = lax.ppermute(side, "dp", mates)
    images, ends, shift = first_step(
        labels, raw, means, mate, side, other, masks, start_basis, spread
    )
    joins = masks[0:1], masks[1:2]
    even, *ups = (masks[i : i + 1] > 0.5 for i in range(8, 11))
    bits = {1 << b: masks[10 + b : 11 + b] > 0.5 for b in range(1, 6)}
    masks = tuple(masks[i : i + 1] for i in range(2, 6))
    sides = [(origins[i : i + 1], origins[i + 1 : i + 2]) for i in (0, 2)]

    def exchange(ends, mate=None, beside=lambda: ()):
        mate, own = mate or swap(ends), halves(ends)
        totals = chip_totals(own, mate, joins, even)
        arrived = [
            lax.ppermute(jnp.where(up, totals[1], totals[0]), "dp", link) for link, up in zip(links, ups)
        ]
        arrived, other = lax.optimization_barrier((arrived, beside()))
        left = right = jnp.zeros_like(own[0])
        for got, (from_left, from_right) in zip(arrived, sides):
            left = left + from_left * got
            right = right + from_right * got
        return *collect(left, right, own, mate, masks), other

    def halve(tiles, bit):
        low, high = tiles[0::2], tiles[1::2]
        set_here = bits[bit]
        return jnp.where(set_here, high, low), jnp.where(set_here, low, high)

    def route(sent, bit):
        return lax.ppermute(sent, "dp", [(i, i ^ bit) for i in range(n_dp)])

    def split(tiles, bit):
        kept, sent = halve(tiles, bit)
        return kept + route(sent, bit)

    for _ in range(ITERS - 3):
        images, ends = step(labels, images, *exchange(ends)[:2], shift, spread)

    images, ends, kept = step_and_route(
        owner_table, place, labels, images, *exchange(ends)[:2], shift, spread
    )
    got = lax.ppermute(ends, "dp", mates)
    kept = (kept + got[2 * DIRS :]).reshape(n_dp // 2, DIRS, width)
    kept, sent = halve(kept, 2)
    first, last_image, got = exchange(ends[: 2 * DIRS], halves(got[: 2 * DIRS]), lambda: route(sent, 2))
    kept = kept + got
    bit = 4
    while 2 * bit < n_dp:
        kept = split(kept, bit)
        bit *= 2
    kept, sent = halve(kept, bit)
    got = route(sent, bit)
    projections = project(labels, images, first, last_image, means, shift, rows_here)
    return finish(kept, got), projections


def solution(mesh):
    in_specs = (P(("groups", "dp"), None), P(("groups", "dp")), P("groups"), P())
    out_specs = (P(("groups", "dp"), None, None), P(None, ("groups", "dp")))
    body = functools.partial(per_device, mesh.shape["dp"])
    return jax.shard_map(body, mesh=mesh, in_specs=in_specs, out_specs=out_specs, check_vma=False)
```
